512 devices in a mesh: span: 8 (over z_hi, y), stream: 64 (over x, z_lo, core).
Axes of the slice: x: 4, y: 4, z: 16 (z_hi: 2, z_lo: 8; z = z_hi * 8 + z_lo), core: 2. Of those that a mesh axis runs over, the one named last changes fastest.
Arguments:
- velocity: float32 [3, 32, 512, 256], P(None, 'span', 'stream'), may hold values from -32 to 32
- strain: float32 [6, 32, 512, 256], P(None, 'span', 'stream'), may hold values from -4 to 4
- row_bins: int32 [512], P('stream'), may hold values from 0 to 63, never falling along the last dimension, each value on 1 to 16 neighbouring positions
- cotangent: float32 [6, 32, 512, 256], P(None, 'span', 'stream'), may hold values from -6 to 6
Outputs:
- model_residual: float32 [6, 32, 512, 256], P(None, 'span', 'stream')
- velocity_grad: float32 [3, 32, 512, 256], P(None, 'span', 'stream')
The draws below stay inside these ranges and needn't reach their ends.
Inputs may be any that keep to these rules, and one draw needn't show every extreme that they name: `row_bins`: bins never fall along the rows, and every bin holds 1 to 16 rows.
All inputs are finite; a program needn't handle non-finite values.
Results may differ from the reference program's by a relative error of at most 0.0003.
Values sent between devices are 32-bit elements; how exact they have to be, the bound alone decides.
A program may use at most 64 MiB of HBM per device.

```python
import math
import jax
import jax.numpy as jnp
import numpy as np
from jax import lax

PX = 256
NBINS = 64
NZ = 32
NY = 512


def draw_velocity(key, part):
    key_base, key_span, key_plane = jax.random.split(key, 3)
    span_scale = jnp.exp(jax.random.uniform(key_span, (1, NZ, 1, 1), minval=-0.7, maxval=0.7))
    plane_scale = jnp.exp(jax.random.uniform(key_plane, (1, 1, 1, PX), minval=-0.7, maxval=0.7))
    row_positions = jnp.arange(NY, dtype=jnp.float32)
    row_scale = (0.6 * jnp.exp(jnp.log(3.0) * row_positions / NY))[None, None, :, None]
    base_draw = jnp.clip(jax.random.normal(key_base, (3, NZ, NY, PX)), -4.0, 4.0)
    return (base_draw * span_scale * plane_scale * row_scale).astype(jnp.float32)


def steps_of(key, dims, cuts, smallest, high):
    def one(dim, shards_of):
        heights = jax.random.uniform(jax.random.fold_in(jax.random.fold_in(key, 6), dim), (shards_of,), jnp.float32, smallest / len(cuts), high / len(cuts))
        return jnp.repeat(jnp.exp(heights), dims[dim] // shards_of).reshape((-1,) + (1,) * (len(dims) - dim - 1))

    gain = one(*cuts[0])
    for cut in cuts[1:]:
        gain = gain * one(*cut)
    return gain


def length_profile(number_of, total, limit, slope):
    loads = [(1 << 20) // math.isqrt(grade ** slope) + 1 for grade in range(2, number_of + 1)]
    surplus, holding = total - limit - (number_of - 1), [1] * (number_of - 1)
    while surplus > 0:
        free = [i for i in range(number_of - 1) if holding[i] < limit]
        mass, remaining = sum([loads[i] for i in free]), surplus
        for i in free:
            addition = min(limit - holding[i], max(1, remaining * loads[i] // mass), surplus)
            holding[i] = holding[i] + addition
            surplus = surplus - addition
    return np.array([limit] + holding)


def ragged(stream_key, number_of, total, most, lean):
    if number_of == 2:
        one = jax.random.randint(stream_key, (), max(1, total - most), min(most, total - 1) + 1)
        return jnp.stack([one, total - one])
    sizes = jnp.asarray(length_profile(number_of, total, most, lean), jnp.int32)
    couples = (number_of - 1) // 2
    giver, taker = sizes[1:1 + 2 * couples:2], sizes[2:2 + 2 * couples:2]
    room = jnp.minimum(giver - 1, most - taker)
    shifted = jax.random.randint(jax.random.fold_in(stream_key, 1), (couples,), 0, 1 << 20) % (room + 1)
    sizes = sizes.at[1:1 + 2 * couples:2].set(giver - shifted).at[2:2 + 2 * couples:2].set(taker + shifted)
    return sizes[jax.random.permutation(jax.random.fold_in(stream_key, 2), number_of)]


def noise(stream_key, dims, scale, most, pieces=(), held_as=jnp.bfloat16):
    factor_of = steps_of(stream_key, dims, pieces, -0.22, 0.18) if pieces else 1.0
    entries = jax.random.normal(stream_key, dims, jnp.float32) * scale * factor_of
    return jnp.minimum(jnp.maximum(entries, -most), most).astype(held_as)


def setup_inputs(seed: int = 0) -> dict:
    arg_keys = jax.random.split(jax.random.key(seed), 5)
    return {
        "velocity": draw_velocity(jax.random.fold_in(arg_keys[4], 71), 0),
        "strain": noise(arg_keys[1], (6, NZ, NY, PX), 0.3, 4.0, ((1, 8), (2, 64)), jnp.float32),
        "row_bins": jnp.searchsorted(jnp.cumsum(ragged(arg_keys[2], NBINS, NY, 2 * NY // NBINS, 0)), jnp.arange(NY), side="right").astype(jnp.int32),
        "cotangent": noise(arg_keys[3], (6, NZ, NY, PX), 1.0, 6.0, ((1, 8), (2, 64)), jnp.float32),
    }


FILTER_ALPHA = 0.45
CENTER_WEIGHT = 0.95
SIDE_WEIGHT = 0.475
STRAIN_FLOOR = 0.25
EPSILON = 1e-06
INDEX_PAIRS = ((0, 0), (0, 1), (0, 2), (1, 1), (1, 2), (2, 2))
PAIR_WEIGHTS = (1.0, 2.0, 2.0, 1.0, 2.0, 1.0)
HIGHEST = lax.Precision.HIGHEST

def explicit_side(values):
    return CENTER_WEIGHT * values + SIDE_WEIGHT * (jnp.roll(values, 1, axis=1) + jnp.roll(values, -1, axis=1))

def implicit_inverse(cell_count):
    identity = jnp.eye(cell_count, dtype=jnp.float32)
    system = identity + FILTER_ALPHA * (jnp.roll(identity, 1, axis=1) + jnp.roll(identity, -1, axis=1))
    return jnp.linalg.inv(system)

def test_filter(values, inverse):
    return jnp.einsum('zw,fwyx->fzyx', inverse, explicit_side(values), precision=HIGHEST)

def germano(velocity, strain, row_bins):
    inverse = implicit_inverse(velocity.shape[1])
    onehot = (row_bins[:, None] == jnp.arange(NBINS, dtype=jnp.int32)[None, :]).astype(jnp.float32)
    weights = jnp.asarray(PAIR_WEIGHTS, jnp.float32)[:, None, None, None]
    products = jnp.stack([velocity[former] * velocity[latter] for former, latter in INDEX_PAIRS])
    size_field = jnp.sqrt(jnp.maximum(2.0 * lax.optimization_barrier(jnp.sum(weights * strain * strain, axis=0)), STRAIN_FLOOR))
    fields = jnp.concatenate([velocity, products, size_field[None]], axis=0)
    filtered = test_filter(fields, inverse)
    coarse = jnp.stack([filtered[former] * filtered[latter] for former, latter in INDEX_PAIRS])
    leonard = filtered[3:9] - coarse
    model_term = products - coarse + 2.0 * (4.0 * filtered[9] - size_field)[None] * strain
    cross_rows = lax.optimization_barrier(jnp.sum(weights * leonard * model_term, axis=(0, 1, 3)))
    square_rows = lax.optimization_barrier(jnp.sum(weights * model_term * model_term, axis=(0, 1, 3)))
    numerator = jnp.dot(cross_rows, onehot, precision=HIGHEST)
    denominator = jnp.dot(square_rows, onehot, precision=HIGHEST) + EPSILON
    coefficient = numerator / denominator
    row_coefficient = jnp.dot(onehot, coefficient, precision=HIGHEST)
    return leonard - row_coefficient[None, None, :, None] * model_term

def reference(velocity, strain, row_bins, cotangent):
    residual, pullback = jax.vjp(lambda moving: germano(moving, strain, row_bins), velocity)
    return (residual, pullback(cotangent)[0])
```

```python
import jax
import jax.numpy as jnp
from jax import lax
from jax.experimental import pallas as pl
from jax.experimental.pallas import tpu as pltpu
from jax.sharding import PartitionSpec as P

ALPHA = 0.45
CENTER_WEIGHT = 0.95
SIDE_WEIGHT = 0.475
STRAIN_FLOOR = 0.25
EPSILON = 1e-06
PAIRS = ((0, 0), (0, 1), (0, 2), (1, 1), (1, 2), (2, 2))
WEIGHTS = (1.0, 2.0, 2.0, 1.0, 2.0, 1.0)
MESH = pl.DeviceIdType.MESH

ROOT = ((1.0 - 4.0 * ALPHA * ALPHA) ** 0.5 - 1.0) / (2.0 * ALPHA)
GREEN = 1.0 / (1.0 - 4.0 * ALPHA * ALPHA) ** 0.5
SCALE = SIDE_WEIGHT / ALPHA
REST = SCALE - CENTER_WEIGHT
OWN = SCALE + REST * GREEN
SWEEP = -REST * GREEN
CELLS, RING, GROUPS = 4, 4, 2
STEP = ROOT ** CELLS
AROUND = STEP ** RING
CLOSE = 1.0 / (1.0 - AROUND**GROUPS)
STREAM_STEPS = (-2, -1, 1, 2)


def ends(cells):
    right, left = cells[0], cells[3]
    for i in (1, 2, 3):
        right = cells[i] + ROOT * right
        left = cells[3 - i] + ROOT * left
    return right, left


def filtered_cells(cells, before, after):
    up, down = [], []
    for i in range(CELLS):
        before = cells[i] + ROOT * before
        after = cells[CELLS - 1 - i] + ROOT * after
        up.append(before)
        down.append(after)
    return [OWN * cells[i] + SWEEP * (up[i] + down[CELLS - 1 - i]) for i in range(CELLS)]


def carry(blocks):
    total = blocks[0]
    for p in (1, 2, 3):
        total = blocks[p] + STEP * total
    return total


def kernel(vel, strain, bins, cot, res, grad,
           fields, filt, leo, mod, back,
           e1, rb1, pa1, zb1, g1, ag1,
           ec, rbc, pac, zbc,
           e2, rb2, pa2, zb2, g2, ag2,
           t1, ty, t2, ts, t3, tz,
           send, recv):
    span, stream = lax.axis_index("span"), lax.axis_index("stream")
    h, y = span // RING, lax.rem(span, RING)
    mirror = lax.rem(y, 2)
    place = y + mirror * (RING - 1 - 2 * y)

    def ring_peer(delta):
        return lax.rem(y + delta, RING)

    def ring_id(other):
        return (h * RING + other, stream)

    across = ((GROUPS - 1 - h) * RING + y, stream)

    def stream_id(step):
        turn = (lax.rem(stream, 16) + step + 16) // 16 - 1
        flip = turn * turn
        return ((h + flip - 2 * h * flip) * RING + y, lax.rem(stream + step + 64, 64))

    copies = []

    def push(src, dst, device):
        n = len(copies)
        copy = pltpu.make_async_remote_copy(
            src_ref=src, dst_ref=dst, send_sem=send.at[n], recv_sem=recv.at[n],
            device_id=device, device_id_type=MESH)
        copy.start()
        copies.append(copy)
        return copy

    def scatter(src, dst):
        out = []
        for delta in (2, 1, 3):
            other = ring_peer(delta)
            slot = y + lax.rem(other, 2) * (RING - 1 - 2 * y)
            out.append(push(src.at[other], dst.at[slot], ring_id(other)))
        dst[place] = src[y]
        return out

    def spread(src, dst):
        out = []
        for delta in (2, 1, 3):
            other = ring_peer(delta)
            slot = other + mirror * (RING - 1 - 2 * other)
            out.append(push(src.at[slot], dst.at[y], ring_id(other)))
        dst[y] = src[place]
        return out

    def arrive(group):
        for copy in group:
            copy.wait_recv()

    def keep_ends(buf, at, cells):
        right, left = ends(cells)
        for half in (0, 1):
            lanes = slice(128 * half, 128 * half + 128)
            buf[2 * half, at] = right[..., lanes]
            buf[2 * half + 1, at] = left[..., lanes]

    barrier = pltpu.get_barrier_semaphore()
    greeted = [ring_id(ring_peer(d)) for d in (1, 2, 3)] + [across] + [stream_id(s) for s in STREAM_STEPS]
    for device in greeted:
        pl.semaphore_signal(barrier, inc=1, device_id=device, device_id_type=MESH)

    for a in range(3):
        fields[a] = vel[a]
    total = jnp.zeros((CELLS, 8, 256), jnp.float32)
    for k, (a, b) in enumerate(PAIRS):
        fields[3 + k] = vel[a] * vel[b]
        total = total + WEIGHTS[k] * (strain[k] * strain[k])
    fields[9] = jnp.sqrt(jnp.maximum(2.0 * total, STRAIN_FLOOR))
    for f in range(10):
        keep_ends(e1, f, [fields[f, i] for i in range(CELLS)])
    for k in range(6):
        keep_ends(ec, k, [cot[k, i] for i in range(CELLS)])
    row = lax.broadcasted_iota(jnp.int32, (8, 128), 0)
    lane = lax.broadcasted_iota(jnp.int32, (8, 128), 1)
    own_bins = jnp.zeros((8, 128), jnp.float32)
    for i in range(8):
        own_bins = jnp.where(row == i, bins[i].astype(jnp.float32), own_bins)

    pl.semaphore_wait(barrier, len(greeted))

    first = scatter(e1, rb1)
    first_cot = scatter(ec, rbc)
    arrive(first)
    pa1[...] = carry([rb1[p] for p in range(RING)])
    over = push(pa1, zb1, across)
    arrive(first_cot)
    pac[...] = carry([rbc[p] for p in range(RING)])
    over_cot = push(pac, zbc, across)
    arrive([over])
    entering = CLOSE * (zb1[...] + AROUND * pa1[...])
    g1[0] = entering
    for p in range(RING - 1):
        entering = rb1[p] + STEP * entering
        g1[p + 1] = entering
    arrive(spread(g1, ag1))

    for f in (9, 0, 1, 2):
        for half in (0, 1):
            lanes = slice(128 * half, 128 * half + 128)
            out = filtered_cells([fields[f, i, :, lanes] for i in range(CELLS)],
                                 ag1[2 * half, f], ag1[2 * half + 1, f])
            for i in range(CELLS):
                filt[f % 9 if f < 9 else 3, i, :, lanes] = out[i]
    cross = jnp.zeros((8, 256), jnp.float32)
    square = jnp.zeros((8, 256), jnp.float32)
    blame = jnp.zeros((8, 256), jnp.float32)
    for k, (a, b) in enumerate(PAIRS):
        f = 3 + k
        halves = []
        for half in (0, 1):
            lanes = slice(128 * half, 128 * half + 128)
            halves.append(filtered_cells([fields[f, i, :, lanes] for i in range(CELLS)],
                                         ag1[2 * half, f], ag1[2 * half + 1, f]))
        for i in range(CELLS):
            coarse = filt[a, i] * filt[b, i]
            leonard = jnp.concatenate([halves[0][i], halves[1][i]], axis=-1) - coarse
            size = fields[9, i]
            model = fields[f, i] - coarse + 2.0 * (4.0 * filt[3, i] - size) * strain[k, i]
            leo[k, i] = leonard
            mod[k, i] = model
            cross = cross + WEIGHTS[k] * (leonard * model)
            square = square + WEIGHTS[k] * (model * model)
            blame = blame + cot[k, i] * model

    def over_lanes(values):
        return jnp.sum(values[:, :128] + values[:, 128:], axis=-1, keepdims=True)

    t1[...] = jnp.where(lane == 0, over_lanes(cross),
                        jnp.where(lane == 1, over_lanes(square),
                                  jnp.where(lane == 2, over_lanes(blame), own_bins)))
    rows_out = [push(t1, ty.at[d - 1], ring_id(ring_peer(d))) for d in (2, 1, 3)]

    for k in range(6):
        keep_ends(e2, k, [WEIGHTS[k] * mod[k, i] for i in range(CELLS)])
    for a in range(3):
        with_cot, with_sum, with_model = [], [], []
        for i in range(CELLS):
            u = v = w = None
            for k, (former, latter) in enumerate(PAIRS):
                if a not in (former, latter):
                    continue
                other = latter if former == a else former
                factor = filt[other, i] * (2.0 if former == latter else 1.0)
                weighted = WEIGHTS[k] * factor
                terms = (cot[k, i] * factor, (mod[k, i] + leo[k, i]) * weighted, mod[k, i] * weighted)
                u, v, w = terms if u is None else (u + terms[0], v + terms[1], w + terms[2])
            with_cot.append(u)
            with_sum.append(v)
            with_model.append(w)
            back[0, a, i] = u
            back[1, a, i] = v
            back[2, a, i] = w
        keep_ends(e2, 6 + a, with_cot)
        keep_ends(e2, 9 + a, with_sum)
        keep_ends(e2, 12 + a, with_model)
    second = scatter(e2, rb2)

    arrive(rows_out)
    t2[...] = jnp.where(lane == 3, own_bins, t1[...] + ty[0] + ty[1] + ty[2])
    near = [push(t2, ts.at[n], stream_id(s)) for n, s in enumerate(STREAM_STEPS)]
    arrive(second)
    pa2[...] = carry([rb2[p] for p in range(RING)])
    over2 = push(pa2, zb2, across)
    arrive(near)
    sums = jnp.zeros((8, 128), jnp.float32)
    for n in range(5):
        tile = t2[...] if n == 4 else ts[n]
        tile_bins = jnp.broadcast_to(tile[:, 3:4], (8, 128))
        for j in range(8):
            sums = sums + jnp.where(own_bins == tile_bins[j:j + 1], tile[j:j + 1], 0.0)
    t3[...] = sums
    over3 = push(t3, tz, across)
    arrive([over3])
    sums = sums + tz[...]
    denominator = jnp.broadcast_to(sums[:, 1:2], (8, 128)) + EPSILON
    coefficient = jnp.broadcast_to(sums[:, 0:1], (8, 128)) / denominator
    row_cross = -jnp.broadcast_to(sums[:, 2:3], (8, 128)) / denominator
    row_square = -2.0 * row_cross * coefficient
    spare = coefficient - 1.0

    def combined(part, part_cot):
        coarse = spare * part(6, 9) - row_cross * part(9, 12) - row_square * part(12, 15)
        return coarse, part_cot() + row_cross * part(0, 6)

    arrive([over_cot, over2])
    blocks = [combined(lambda m, n, p=p: rb2[p, m:n], lambda p=p: rbc[p]) for p in range(RING)]
    others = combined(lambda m, n: zb2[m:n], lambda: zbc[...])
    for part, at in ((0, slice(0, 3)), (1, slice(3, 9))):
        entering = CLOSE * (others[part] + AROUND * carry([block[part] for block in blocks]))
        g2[0, at] = entering
        for p in range(RING - 1):
            entering = blocks[p][part] + STEP * entering
            g2[p + 1, at] = entering
    last = spread(g2, ag2)

    def wide(values):
        return jnp.concatenate([values, values], axis=-1)

    coefficient, row_cross, row_square, spare = (
        wide(coefficient), wide(row_cross), wide(row_square), wide(spare))
    for a in range(3):
        for i in range(CELLS):
            back[0, a, i] = spare * back[0, a, i] - row_cross * back[1, a, i] - row_square * back[2, a, i]
    for k in range(6):
        for i in range(CELLS):
            leonard, model, bar = leo[k, i], mod[k, i], cot[k, i]
            res[k, i] = leonard - coefficient * model
            weighted = WEIGHTS[k] * row_cross
            leo[k, i] = bar + weighted * model
            mod[k, i] = weighted * leonard - coefficient * bar + (WEIGHTS[k] * row_square) * model
    arrive(last)
    for half in (0, 1):
        lanes = slice(128 * half, 128 * half + 128)
        sums = []
        for a in range(3):
            sums.append(filtered_cells([back[0, a, i, :, lanes] for i in range(CELLS)],
                                       ag2[2 * half, a], ag2[2 * half + 1, a]))
        for k, (a, b) in enumerate(PAIRS):
            pulled = filtered_cells([leo[k, i, :, lanes] for i in range(CELLS)],
                                    ag2[2 * half, 3 + k], ag2[2 * half + 1, 3 + k])
            for i in range(CELLS):
                through = pulled[i] + mod[k, i, :, lanes]
                sums[a][i] = sums[a][i] + through * vel[b, i, :, lanes]
                sums[b][i] = sums[b][i] + through * vel[a, i, :, lanes]
        for a in range(3):
            for i in range(CELLS):
                grad[a, i, :, lanes] = sums[a][i]
    for copy in copies:
        copy.wait_send()


def on_device(velocity, strain, row_bins, cotangent):
    def buf(*shape):
        return pltpu.VMEM(shape, jnp.float32)

    vmem = pl.BlockSpec(memory_space=pltpu.VMEM)
    scratch = [
        buf(10, 4, 8, 256), buf(4, 4, 8, 256), buf(6, 4, 8, 256), buf(6, 4, 8, 256), buf(3, 3, 4, 8, 256),
        buf(4, 10, 8, 128), buf(4, 10, 8, 128), buf(10, 8, 128), buf(10, 8, 128), buf(4, 10, 8, 128),
        buf(4, 10, 8, 128),
        buf(4, 6, 8, 128), buf(4, 6, 8, 128), buf(6, 8, 128), buf(6, 8, 128),
        buf(4, 15, 8, 128), buf(4, 15, 8, 128), buf(15, 8, 128), buf(15, 8, 128), buf(4, 9, 8, 128),
        buf(4, 9, 8, 128),
        buf(8, 128), buf(3, 8, 128), buf(8, 128), buf(4, 8, 128), buf(8, 128), buf(8, 128),
        pltpu.SemaphoreType.DMA((32,)), pltpu.SemaphoreType.DMA((32,)),
    ]
    return pl.pallas_call(
        kernel,
        out_shape=(
            jax.ShapeDtypeStruct(strain.shape, jnp.float32),
            jax.ShapeDtypeStruct(velocity.shape, jnp.float32),
        ),
        in_specs=[vmem, vmem, pl.BlockSpec(memory_space=pltpu.SMEM), vmem],
        out_specs=(vmem, vmem),
        scratch_shapes=scratch,
        compiler_params=pltpu.CompilerParams(
            collective_id=1, has_side_effects=True, vmem_limit_bytes=32 * 1024 * 1024),
        cost_estimate=pl.CostEstimate(flops=3_000_000, bytes_accessed=800_000, transcendentals=8192),
    )(velocity, strain, row_bins, cotangent)


def solution(mesh):
    field = P(None, "span", "stream", None)
    return jax.shard_map(
        on_device, mesh=mesh, in_specs=(field, field, P("stream"), field), out_specs=(field, field),
        check_vma=False)
```

```python
import jax
import jax.numpy as jnp
from jax import lax
from jax.experimental import pallas as pl
from jax.experimental.pallas import tpu as pltpu
from jax.sharding import PartitionSpec as P

ALPHA = 0.45
CENTER_WEIGHT = 0.95
SIDE_WEIGHT = 0.475
STRAIN_FLOOR = 0.25
EPSILON = 1e-06
PAIRS = ((0, 0), (0, 1), (0, 2), (1, 1), (1, 2), (2, 2))
WEIGHTS = (1.0, 2.0, 2.0, 1.0, 2.0, 1.0)
MESH = pl.DeviceIdType.MESH

ROOT = ((1.0 - 4.0 * ALPHA * ALPHA) ** 0.5 - 1.0) / (2.0 * ALPHA)
GREEN = 1.0 / (1.0 - 4.0 * ALPHA * ALPHA) ** 0.5
SCALE = SIDE_WEIGHT / ALPHA
REST = SCALE - CENTER_WEIGHT
OWN = SCALE + REST * GREEN
SWEEP = -REST * GREEN
CELLS, RING, GROUPS = 4, 4, 2
STEP = ROOT ** CELLS
AROUND = STEP ** RING
CLOSE = 1.0 / (1.0 - AROUND**GROUPS)
STREAM_STEPS = (-2, -1, 1, 2)


def ends(cells):
    right, left = cells[0], cells[3]
    for i in (1, 2, 3):
        right = cells[i] + ROOT * right
        left = cells[3 - i] + ROOT * left
    return right, left


def filtered_cells(cells, before, after):
    up, down = [], []
    for i in range(CELLS):
        before = cells[i] + ROOT * before
        after = cells[CELLS - 1 - i] + ROOT * after
        up.append(before)
        down.append(after)
    return [OWN * cells[i] + SWEEP * (up[i] + down[CELLS - 1 - i]) for i in range(CELLS)]


def carry(blocks):
    total = blocks[0]
    for p in (1, 2, 3):
        total = blocks[p] + STEP * total
    return total


def kernel(vel_in, strain_in, bins_in, cot_in, res, grad,
           vel, strain, bins, cot, fields, filt, leo, mod, back,
           e1, rb1, pa1, zb1, g1, ag1,
           ec, rbc, pac, zbc,
           e2, rb2, pa2, zb2, g2, ag2,
           t1, ty, t2, ts, t3, tz,
           send, recv, load, gate):
    span, stream = lax.axis_index("span"), lax.axis_index("stream")
    h, y = span // RING, lax.rem(span, RING)
    mirror = lax.rem(y, 2)
    place = y + mirror * (RING - 1 - 2 * y)

    def ring_peer(delta):
        return lax.rem(y + delta, RING)

    def ring_id(other):
        return (h * RING + other, stream)

    across = ((GROUPS - 1 - h) * RING + y, stream)

    def stream_id(step):
        turn = (lax.rem(stream, 16) + step + 16) // 16 - 1
        flip = turn * turn
        return ((h + flip - 2 * h * flip) * RING + y, lax.rem(stream + step + 64, 64))

    copies = []

    def push(src, dst, device):
        n = len(copies)
        copy = pltpu.make_async_remote_copy(
            src_ref=src, dst_ref=dst, send_sem=send.at[n], recv_sem=recv.at[n],
            device_id=device, device_id_type=MESH)
        copy.start()
        copies.append(copy)
        return copy

    def scatter(src, dst):
        out = []
        for delta in (2, 1, 3):
            other = ring_peer(delta)
            slot = y + lax.rem(other, 2) * (RING - 1 - 2 * y)
            out.append(push(src.at[other], dst.at[slot], ring_id(other)))
        dst[place] = src[y]
        return out

    def spread(src, dst):
        out = []
        for delta in (2, 1, 3):
            other = ring_peer(delta)
            slot = other + mirror * (RING - 1 - 2 * other)
            out.append(push(src.at[slot], dst.at[y], ring_id(other)))
        dst[y] = src[place]
        return out

    def arrive(group):
        for copy in group:
            copy.wait_recv()

    def keep_ends(buf, at, cells):
        right, left = ends(cells)
        for half in (0, 1):
            lanes = slice(128 * half, 128 * half + 128)
            buf[2 * half, at] = right[..., lanes]
            buf[2 * half + 1, at] = left[..., lanes]

    core = lax.rem(stream, 2)
    this_chip = stream - core

    def greet(sem, device):
        pl.semaphore_signal(sem, inc=1, device_id=device, device_id_type=MESH)

    def chip_id(step):
        there, position = stream_id(2 * step)
        return (there, position - core)

    barrier = pltpu.get_barrier_semaphore()
    greet(barrier, (across[0], this_chip))
    for d in (2, 1, 3):
        greet(barrier, (h * RING + ring_peer(d), this_chip + 1))
    greet(barrier, chip_id(-1))
    greet(barrier, chip_id(1))

    @pl.when(core == 0)
    def _():
        greet(barrier, (span, stream + 1))

    loads = [pltpu.make_async_copy(src, dst, load.at[n]) for n, (src, dst) in enumerate(
        ((vel_in, vel), (strain_in, strain), (cot_in, cot), (bins_in, bins)))]
    for one in loads:
        one.start()
    for one in loads:
        one.wait()

    for a in range(3):
        fields[a] = vel[a]
    total = jnp.zeros((CELLS, 8, 256), jnp.float32)
    for k, (a, b) in enumerate(PAIRS):
        fields[3 + k] = vel[a] * vel[b]
        total = total + WEIGHTS[k] * (strain[k] * strain[k])
    fields[9] = jnp.sqrt(jnp.maximum(2.0 * total, STRAIN_FLOOR))
    for f in range(10):
        keep_ends(e1, f, [fields[f, i] for i in range(CELLS)])
    for k in range(6):
        keep_ends(ec, k, [cot[k, i] for i in range(CELLS)])
    row = lax.broadcasted_iota(jnp.int32, (8, 128), 0)
    lane = lax.broadcasted_iota(jnp.int32, (8, 128), 1)
    own_bins = jnp.zeros((8, 128), jnp.float32)
    for i in range(8):
        own_bins = jnp.where(row == i, bins[i].astype(jnp.float32), own_bins)

    @pl.when(core == 1)
    def _():
        pl.semaphore_wait(barrier, 2 * (RING - 1) + 1)
        greet(gate, (span, stream - 1))

    @pl.when(core == 0)
    def _():
        pl.semaphore_wait(gate, 1)

    first = scatter(e1, rb1)
    first_cot = scatter(ec, rbc)
    arrive(first)
    pa1[...] = carry([rb1[p] for p in range(RING)])

    @pl.when(core == 0)
    def _():
        pl.semaphore_wait(barrier, 2 + 2 * 2)
        greet(gate, (span, stream + 1))

    @pl.when(core == 1)
    def _():
        pl.semaphore_wait(gate, 1)

    over = push(pa1, zb1, across)
    arrive(first_cot)
    pac[...] = carry([rbc[p] for p in range(RING)])
    over_cot = push(pac, zbc, across)
    arrive([over])
    entering = CLOSE * (zb1[...] + AROUND * pa1[...])
    g1[0] = entering
    for p in range(RING - 1):
        entering = rb1[p] + STEP * entering
        g1[p + 1] = entering
    arrive(spread(g1, ag1))

    for f in (9, 0, 1, 2):
        for half in (0, 1):
            lanes = slice(128 * half, 128 * half + 128)
            out = filtered_cells([fields[f, i, :, lanes] for i in range(CELLS)],
                                 ag1[2 * half, f], ag1[2 * half + 1, f])
            for i in range(CELLS):
                filt[f % 9 if f < 9 else 3, i, :, lanes] = out[i]
    cross = jnp.zeros((8, 256), jnp.float32)
    square = jnp.zeros((8, 256), jnp.float32)
    blame = jnp.zeros((8, 256), jnp.float32)
    for k, (a, b) in enumerate(PAIRS):
        f = 3 + k
        halves = []
        for half in (0, 1):
            lanes = slice(128 * half, 128 * half + 128)
            halves.append(filtered_cells([fields[f, i, :, lanes] for i in range(CELLS)],
                                         ag1[2 * half, f], ag1[2 * half + 1, f]))
        for i in range(CELLS):
            coarse = filt[a, i] * filt[b, i]
            leonard = jnp.concatenate([halves[0][i], halves[1][i]], axis=-1) - coarse
            size = fields[9, i]
            model = fields[f, i] - coarse + 2.0 * (4.0 * filt[3, i] - size) * strain[k, i]
            leo[k, i] = leonard
            mod[k, i] = model
            cross = cross + WEIGHTS[k] * (leonard * model)
            square = square + WEIGHTS[k] * (model * model)
            blame = blame + cot[k, i] * model

    def over_lanes(values):
        return jnp.sum(values[:, :128] + values[:, 128:], axis=-1, keepdims=True)

    t1[...] = jnp.where(lane == 0, over_lanes(cross),
                        jnp.where(lane == 1, over_lanes(square),
                                  jnp.where(lane == 2, over_lanes(blame), own_bins)))
    rows_out = [push(t1, ty.at[d - 1], ring_id(ring_peer(d))) for d in (2, 1, 3)]

    for k in range(6):
        keep_ends(e2, k, [WEIGHTS[k] * mod[k, i] for i in range(CELLS)])
    for a in range(3):
        with_cot, with_sum, with_model = [], [], []
        for i in range(CELLS):
            u = v = w = None
            for k, (former, latter) in enumerate(PAIRS):
                if a not in (former, latter):
                    continue
                other = latter if former == a else former
                factor = filt[other, i] * (2.0 if former == latter else 1.0)
                weighted = WEIGHTS[k] * factor
                terms = (cot[k, i] * factor, (mod[k, i] + leo[k, i]) * weighted, mod[k, i] * weighted)
                u, v, w = terms if u is None else (u + terms[0], v + terms[1], w + terms[2])
            with_cot.append(u)
            with_sum.append(v)
            with_model.append(w)
            back[0, a, i] = u
            back[1, a, i] = v
            back[2, a, i] = w
        keep_ends(e2, 6 + a, with_cot)
        keep_ends(e2, 9 + a, with_sum)
        keep_ends(e2, 12 + a, with_model)
    second = scatter(e2, rb2)

    arrive(rows_out)
    t2[...] = jnp.where(lane == 3, own_bins, t1[...] + ty[0] + ty[1] + ty[2])
    near = [push(t2, ts.at[n], stream_id(s)) for n, s in enumerate(STREAM_STEPS)]
    arrive(second)
    pa2[...] = carry([rb2[p] for p in range(RING)])
    over2 = push(pa2, zb2, across)
    arrive(near)
    sums = jnp.zeros((8, 128), jnp.float32)
    for n in range(5):
        tile = t2[...] if n == 4 else ts[n]
        tile_bins = jnp.broadcast_to(tile[:, 3:4], (8, 128))
        for j in range(8):
            sums = sums + jnp.where(own_bins == tile_bins[j:j + 1], tile[j:j + 1], 0.0)
    t3[...] = sums
    over3 = push(t3, tz, across)
    arrive([over3])
    sums = sums + tz[...]
    denominator = jnp.broadcast_to(sums[:, 1:2], (8, 128)) + EPSILON
    coefficient = jnp.broadcast_to(sums[:, 0:1], (8, 128)) / denominator
    row_cross = -jnp.broadcast_to(sums[:, 2:3], (8, 128)) / denominator
    row_square = -2.0 * row_cross * coefficient
    spare = coefficient - 1.0

    def combined(part, part_cot):
        coarse = spare * part(6, 9) - row_cross * part(9, 12) - row_square * part(12, 15)
        return coarse, part_cot() + row_cross * part(0, 6)

    arrive([over_cot, over2])
    blocks = [combined(lambda m, n, p=p: rb2[p, m:n], lambda p=p: rbc[p]) for p in range(RING)]
    others = combined(lambda m, n: zb2[m:n], lambda: zbc[...])
    for part, at in ((0, slice(0, 3)), (1, slice(3, 9))):
        entering = CLOSE * (others[part] + AROUND * carry([block[part] for block in blocks]))
        g2[0, at] = entering
        for p in range(RING - 1):
            entering = blocks[p][part] + STEP * entering
            g2[p + 1, at] = entering
    last = spread(g2, ag2)

    def wide(values):
        return jnp.concatenate([values, values], axis=-1)

    coefficient, row_cross, row_square, spare = (
        wide(coefficient), wide(row_cross), wide(row_square), wide(spare))
    for a in range(3):
        for i in range(CELLS):
            back[0, a, i] = spare * back[0, a, i] - row_cross * back[1, a, i] - row_square * back[2, a, i]
    for k in range(6):
        for i in range(CELLS):
            leonard, model, bar = leo[k, i], mod[k, i], cot[k, i]
            res[k, i] = leonard - coefficient * model
            weighted = WEIGHTS[k] * row_cross
            leo[k, i] = bar + weighted * model
            mod[k, i] = weighted * leonard - coefficient * bar + (WEIGHTS[k] * row_square) * model
    arrive(last)
    for half in (0, 1):
        lanes = slice(128 * half, 128 * half + 128)
        sums = []
        for a in range(3):
            sums.append(filtered_cells([back[0, a, i, :, lanes] for i in range(CELLS)],
                                       ag2[2 * half, a], ag2[2 * half + 1, a]))
        for k, (a, b) in enumerate(PAIRS):
            pulled = filtered_cells([leo[k, i, :, lanes] for i in range(CELLS)],
                                    ag2[2 * half, 3 + k], ag2[2 * half + 1, 3 + k])
            for i in range(CELLS):
                through = pulled[i] + mod[k, i, :, lanes]
                sums[a][i] = sums[a][i] + through * vel[b, i, :, lanes]
                sums[b][i] = sums[b][i] + through * vel[a, i, :, lanes]
        for a in range(3):
            for i in range(CELLS):
                grad[a, i, :, lanes] = sums[a][i]
    for copy in copies:
        copy.wait_send()


def on_device(velocity, strain, row_bins, cotangent):
    def buf(*shape):
        return pltpu.VMEM(shape, jnp.float32)

    vmem = pl.BlockSpec(memory_space=pltpu.VMEM)
    hbm = pl.BlockSpec(memory_space=pltpu.HBM)
    scratch = [
        buf(3, 4, 8, 256), buf(6, 4, 8, 256), pltpu.SMEM((8,), jnp.int32), buf(6, 4, 8, 256),
        buf(10, 4, 8, 256), buf(4, 4, 8, 256), buf(6, 4, 8, 256), buf(6, 4, 8, 256), buf(3, 3, 4, 8, 256),
        buf(4, 10, 8, 128), buf(4, 10, 8, 128), buf(10, 8, 128), buf(10, 8, 128), buf(4, 10, 8, 128),
        buf(4, 10, 8, 128),
        buf(4, 6, 8, 128), buf(4, 6, 8, 128), buf(6, 8, 128), buf(6, 8, 128),
        buf(4, 15, 8, 128), buf(4, 15, 8, 128), buf(15, 8, 128), buf(15, 8, 128), buf(4, 9, 8, 128),
        buf(4, 9, 8, 128),
        buf(8, 128), buf(3, 8, 128), buf(8, 128), buf(4, 8, 128), buf(8, 128), buf(8, 128),
        pltpu.SemaphoreType.DMA((32,)), pltpu.SemaphoreType.DMA((32,)), pltpu.SemaphoreType.DMA((4,)),
        pltpu.SemaphoreType.REGULAR,
    ]
    return pl.pallas_call(
        kernel,
        out_shape=(
            pltpu.VMEM(strain.shape, jnp.float32),
            pltpu.VMEM(velocity.shape, jnp.float32),
        ),
        in_specs=[hbm, hbm, hbm, hbm],
        out_specs=(vmem, vmem),
        scratch_shapes=scratch,
        compiler_params=pltpu.CompilerParams(
            collective_id=1, has_side_effects=True, vmem_limit_bytes=32 * 1024 * 1024),
        cost_estimate=pl.CostEstimate(flops=3_000_000, bytes_accessed=800_000, transcendentals=8192),
    )(*[pltpu.with_memory_space_constraint(v, pltpu.HBM) for v in (velocity, strain, row_bins, cotangent)])


def solution(mesh):
    field = P(None, "span", "stream", None)
    return jax.shard_map(
        on_device, mesh=mesh, in_specs=(field, field, P("stream"), field), out_specs=(field, field),
        check_vma=False)
```

```python
import jax
import jax.numpy as jnp
from jax import lax
from jax.experimental import pallas as pl
from jax.experimental.pallas import tpu as pltpu
from jax.sharding import PartitionSpec as P

ALPHA = 0.45
CENTER_WEIGHT = 0.95
SIDE_WEIGHT = 0.475
STRAIN_FLOOR = 0.25
EPSILON = 1e-06
PAIRS = ((0, 0), (0, 1), (0, 2), (1, 1), (1, 2), (2, 2))
WEIGHTS = (1.0, 2.0, 2.0, 1.0, 2.0, 1.0)
MESH = pl.DeviceIdType.MESH

ROOT = ((1.0 - 4.0 * ALPHA * ALPHA) ** 0.5 - 1.0) / (2.0 * ALPHA)
GREEN = 1.0 / (1.0 - 4.0 * ALPHA * ALPHA) ** 0.5
SCALE = SIDE_WEIGHT / ALPHA
REST = SCALE - CENTER_WEIGHT
OWN = SCALE + REST * GREEN
SWEEP = -REST * GREEN
CELLS, RING, GROUPS = 4, 4, 2
STEP = ROOT ** CELLS
AROUND = STEP ** RING
CLOSE = 1.0 / (1.0 - AROUND**GROUPS)
STREAM_STEPS = (-2, -1, 1, 2)


def ends(cells):
    right, left = cells[0], cells[3]
    for i in (1, 2, 3):
        right = cells[i] + ROOT * right
        left = cells[3 - i] + ROOT * left
    return right, left


def filtered_cells(cells, before, after):
    up, down = [], []
    for i in range(CELLS):
        before = cells[i] + ROOT * before
        after = cells[CELLS - 1 - i] + ROOT * after
        up.append(before)
        down.append(after)
    return [OWN * cells[i] + SWEEP * (up[i] + down[CELLS - 1 - i]) for i in range(CELLS)]


def carry(blocks):
    total = blocks[0]
    for p in (1, 2, 3):
        total = blocks[p] + STEP * total
    return total


def kernel(vel_in, strain_in, bins_in, cot_in, res, grad,
           vel, strain, bins, cot, fields, filt, leo, mod, back,
           e1, rb1, pa1, zb1, g1, ag1,
           ec, rbc, pac, zbc,
           e2, rb2, pa2, zb2, g2, ag2,
           t1, ts, t3, tz,
           send, recv, load, gate):
    span, stream = lax.axis_index("span"), lax.axis_index("stream")
    h, y = span // RING, lax.rem(span, RING)
    mirror = lax.rem(y, 2)
    place = y + mirror * (RING - 1 - 2 * y)

    def ring_peer(delta):
        return lax.rem(y + delta, RING)

    def ring_id(other):
        return (h * RING + other, stream)

    across = ((GROUPS - 1 - h) * RING + y, stream)

    def stream_id(step):
        turn = (lax.rem(stream, 16) + step + 16) // 16 - 1
        flip = turn * turn
        return ((h + flip - 2 * h * flip) * RING + y, lax.rem(stream + step + 64, 64))

    copies = []

    def push(src, dst, device):
        n = len(copies)
        copy = pltpu.make_async_remote_copy(
            src_ref=src, dst_ref=dst, send_sem=send.at[n], recv_sem=recv.at[n],
            device_id=device, device_id_type=MESH)
        copy.start()
        copies.append(copy)
        return copy

    def scatter(src, dst, at):
        out = []
        for delta in (2, 1, 3):
            other = ring_peer(delta)
            slot = y + lax.rem(other, 2) * (RING - 1 - 2 * y)
            out.append(push(src.at[other, at], dst.at[slot, at], ring_id(other)))
        dst[place, at] = src[y, at]
        return out

    def spread(src, dst, at):
        out = []
        for delta in (2, 1, 3):
            other = ring_peer(delta)
            slot = other + mirror * (RING - 1 - 2 * other)
            out.append(push(src.at[slot, at], dst.at[y, at], ring_id(other)))
        dst[y, at] = src[place, at]
        return out

    def arrive(group):
        for copy in group:
            copy.wait_recv()

    def keep_ends(buf, at, cells):
        right, left = ends(cells)
        for half in (0, 1):
            lanes = slice(128 * half, 128 * half + 128)
            buf[2 * half, at] = right[..., lanes]
            buf[2 * half + 1, at] = left[..., lanes]

    core = lax.rem(stream, 2)
    this_chip = stream - core

    def greet(sem, device):
        pl.semaphore_signal(sem, inc=1, device_id=device, device_id_type=MESH)

    def chip_id(step):
        there, position = stream_id(2 * step)
        return (there, position - core)

    barrier = pltpu.get_barrier_semaphore()
    greet(barrier, (across[0], this_chip))
    for d in (2, 1, 3):
        greet(barrier, (h * RING + ring_peer(d), this_chip + 1))
    greet(barrier, chip_id(-1))
    greet(barrier, chip_id(1))

    @pl.when(core == 0)
    def _():
        greet(barrier, (span, stream + 1))

    loads = [pltpu.make_async_copy(src, dst, load.at[n]) for n, (src, dst) in enumerate(
        ((vel_in, vel), (strain_in, strain), (cot_in, cot), (bins_in, bins)))]
    for one in loads:
        one.start()
    for one in loads:
        one.wait()

    for a in range(3):
        fields[a] = vel[a]
    total = jnp.zeros((CELLS, 8, 256), jnp.float32)
    for k, (a, b) in enumerate(PAIRS):
        fields[4 + k] = vel[a] * vel[b]
        total = total + WEIGHTS[k] * (strain[k] * strain[k])
    fields[3] = jnp.sqrt(jnp.maximum(2.0 * total, STRAIN_FLOOR))
    for f in range(10):
        keep_ends(e1, f, [fields[f, i] for i in range(CELLS)])
    row = lax.broadcasted_iota(jnp.int32, (8, 128), 0)
    lane = lax.broadcasted_iota(jnp.int32, (8, 128), 1)
    own_bins = jnp.zeros((8, 128), jnp.float32)
    for i in range(8):
        own_bins = jnp.where(row == i, bins[i].astype(jnp.float32), own_bins)

    @pl.when(core == 1)
    def _():
        pl.semaphore_wait(barrier, 2 * (RING - 1) + 1)
        greet(gate, (span, stream - 1))

    @pl.when(core == 0)
    def _():
        pl.semaphore_wait(gate, 1)

    early, late = slice(0, 4), slice(4, 10)
    scattered = [scatter(e1, rb1, at) for at in (early, late)]
    for k in range(6):
        keep_ends(ec, k, [cot[k, i] for i in range(CELLS)])
    crossed, arrived = [], []
    for at, group in zip((early, late), scattered):
        arrive(group)
        pa1[at] = carry([rb1[p, at] for p in range(RING)])
        if not crossed:
            @pl.when(core == 0)
            def _():
                pl.semaphore_wait(barrier, 2 + 2 * 2)
                greet(gate, (span, stream + 1))

            @pl.when(core == 1)
            def _():
                pl.semaphore_wait(gate, 1)

        crossed.append(push(pa1.at[at], zb1.at[at], across))
    for at, copy in zip((early, late), crossed):
        arrive([copy])
        entering = CLOSE * (zb1[at] + AROUND * pa1[at])
        g1[0, at] = entering
        for p in range(RING - 1):
            entering = rb1[p, at] + STEP * entering
            g1[p + 1, at] = entering
        arrived.append(spread(g1, ag1, at))
    first_cot = scatter(ec, rbc, slice(0, 6))
    arrive(arrived[0])

    for f in (0, 1, 2, 3):
        for half in (0, 1):
            lanes = slice(128 * half, 128 * half + 128)
            out = filtered_cells([fields[f, i, :, lanes] for i in range(CELLS)],
                                 ag1[2 * half, f], ag1[2 * half + 1, f])
            for i in range(CELLS):
                filt[f, i, :, lanes] = out[i]
    arrive(arrived[1])
    cross = jnp.zeros((8, 256), jnp.float32)
    square = jnp.zeros((8, 256), jnp.float32)
    blame = jnp.zeros((8, 256), jnp.float32)
    for k, (a, b) in enumerate(PAIRS):
        f = 4 + k
        halves = []
        for half in (0, 1):
            lanes = slice(128 * half, 128 * half + 128)
            halves.append(filtered_cells([fields[f, i, :, lanes] for i in range(CELLS)],
                                         ag1[2 * half, f], ag1[2 * half + 1, f]))
        for i in range(CELLS):
            coarse = filt[a, i] * filt[b, i]
            leonard = jnp.concatenate([halves[0][i], halves[1][i]], axis=-1) - coarse
            size = fields[3, i]
            model = fields[f, i] - coarse + 2.0 * (4.0 * filt[3, i] - size) * strain[k, i]
            leo[k, i] = leonard
            mod[k, i] = model
            cross = cross + WEIGHTS[k] * (leonard * model)
            square = square + WEIGHTS[k] * (model * model)
            blame = blame + cot[k, i] * model

    for k in range(6):
        keep_ends(e2, k, [WEIGHTS[k] * mod[k, i] for i in range(CELLS)])
    early, late = slice(0, 6), slice(6, 15)
    second = [scatter(e2, rb2, early)]

    def over_lanes(values):
        return jnp.sum(values[:, :128] + values[:, 128:], axis=-1, keepdims=True)

    t1[...] = jnp.where(lane == 0, over_lanes(cross),
                        jnp.where(lane == 1, over_lanes(square),
                                  jnp.where(lane == 2, over_lanes(blame), own_bins)))
    near = [push(t1, ts.at[n], stream_id(s)) for n, s in enumerate(STREAM_STEPS)]
    arrive(first_cot)
    pac[...] = carry([rbc[p] for p in range(RING)])
    over_cot = push(pac, zbc, across)

    for a in range(3):
        with_cot, with_sum, with_model = [], [], []
        for i in range(CELLS):
            u = v = w = None
            for k, (former, latter) in enumerate(PAIRS):
                if a not in (former, latter):
                    continue
                other = latter if former == a else former
                factor = filt[other, i] * (2.0 if former == latter else 1.0)
                weighted = WEIGHTS[k] * factor
                terms = (cot[k, i] * factor, (mod[k, i] + leo[k, i]) * weighted, mod[k, i] * weighted)
                u, v, w = terms if u is None else (u + terms[0], v + terms[1], w + terms[2])
            with_cot.append(u)
            with_sum.append(v)
            with_model.append(w)
            back[0, a, i] = u
            back[1, a, i] = v
            back[2, a, i] = w
        keep_ends(e2, 6 + a, with_cot)
        keep_ends(e2, 9 + a, with_sum)
        keep_ends(e2, 12 + a, with_model)
    second.append(scatter(e2, rb2, late))

    arrive(second[0])
    pa2[early] = carry([rb2[p, early] for p in range(RING)])
    over2 = [push(pa2.at[early], zb2.at[early], across)]
    arrive(near)
    sums = jnp.zeros((8, 128), jnp.float32)
    for n in range(5):
        tile = t1[...] if n == 4 else ts[n]
        tile_bins = jnp.broadcast_to(tile[:, 3:4], (8, 128))
        for j in range(8):
            sums = sums + jnp.where(own_bins == tile_bins[j:j + 1], tile[j:j + 1], 0.0)
    t3[...] = sums
    everywhere = [push(t3, tz.at[d - 1], (lax.rem(span + d, 8), stream)) for d in (4, 3, 5, 2, 6, 1, 7)]
    arrive(second[1])
    pa2[late] = carry([rb2[p, late] for p in range(RING)])
    over2.append(push(pa2.at[late], zb2.at[late], across))
    arrive(everywhere)
    for d in range(7):
        sums = sums + tz[d]
    denominator = jnp.broadcast_to(sums[:, 1:2], (8, 128)) + EPSILON
    coefficient = jnp.broadcast_to(sums[:, 0:1], (8, 128)) / denominator
    row_cross = -jnp.broadcast_to(sums[:, 2:3], (8, 128)) / denominator
    row_square = -2.0 * row_cross * coefficient
    spare = coefficient - 1.0

    def adjoint(at, blocks, other):
        entering = CLOSE * (other + AROUND * carry(blocks))
        g2[0, at] = entering
        for p in range(RING - 1):
            entering = blocks[p] + STEP * entering
            g2[p + 1, at] = entering
        return spread(g2, ag2, at)

    def coarse_part(buf, *p):
        return (spare * buf[(*p, slice(6, 9))] - row_cross * buf[(*p, slice(9, 12))]
                - row_square * buf[(*p, slice(12, 15))])

    arrive([over_cot, over2[0]])
    last = adjoint(slice(3, 9), [rbc[p] + row_cross * rb2[p, 0:6] for p in range(RING)],
                   zbc[...] + row_cross * zb2[0:6])
    arrive([over2[1]])
    last = last + adjoint(slice(0, 3), [coarse_part(rb2, p) for p in range(RING)], coarse_part(zb2))

    def wide(values):
        return jnp.concatenate([values, values], axis=-1)

    coefficient, row_cross, row_square, spare = (
        wide(coefficient), wide(row_cross), wide(row_square), wide(spare))
    for a in range(3):
        for i in range(CELLS):
            back[0, a, i] = spare * back[0, a, i] - row_cross * back[1, a, i] - row_square * back[2, a, i]
    for k in range(6):
        for i in range(CELLS):
            leonard, model, bar = leo[k, i], mod[k, i], cot[k, i]
            res[k, i] = leonard - coefficient * model
            weighted = WEIGHTS[k] * row_cross
            leo[k, i] = bar + weighted * model
            mod[k, i] = weighted * leonard - coefficient * bar + (WEIGHTS[k] * row_square) * model
    arrive(last)
    for half in (0, 1):
        lanes = slice(128 * half, 128 * half + 128)
        sums = []
        for a in range(3):
            sums.append(filtered_cells([back[0, a, i, :, lanes] for i in range(CELLS)],
                                       ag2[2 * half, a], ag2[2 * half + 1, a]))
        for k, (a, b) in enumerate(PAIRS):
            pulled = filtered_cells([leo[k, i, :, lanes] for i in range(CELLS)],
                                    ag2[2 * half, 3 + k], ag2[2 * half + 1, 3 + k])
            for i in range(CELLS):
                through = pulled[i] + mod[k, i, :, lanes]
                sums[a][i] = sums[a][i] + through * vel[b, i, :, lanes]
                sums[b][i] = sums[b][i] + through * vel[a, i, :, lanes]
        for a in range(3):
            for i in range(CELLS):
                grad[a, i, :, lanes] = sums[a][i]
    for copy in copies:
        copy.wait_send()


def on_device(velocity, strain, row_bins, cotangent):
    def buf(*shape):
        return pltpu.VMEM(shape, jnp.float32)

    vmem = pl.BlockSpec(memory_space=pltpu.VMEM)
    hbm = pl.BlockSpec(memory_space=pltpu.HBM)
    scratch = [
        buf(3, 4, 8, 256), buf(6, 4, 8, 256), pltpu.SMEM((8,), jnp.int32), buf(6, 4, 8, 256),
        buf(10, 4, 8, 256), buf(4, 4, 8, 256), buf(6, 4, 8, 256), buf(6, 4, 8, 256), buf(3, 3, 4, 8, 256),
        buf(4, 10, 8, 128), buf(4, 10, 8, 128), buf(10, 8, 128), buf(10, 8, 128), buf(4, 10, 8, 128),
        buf(4, 10, 8, 128),
        buf(4, 6, 8, 128), buf(4, 6, 8, 128), buf(6, 8, 128), buf(6, 8, 128),
        buf(4, 15, 8, 128), buf(4, 15, 8, 128), buf(15, 8, 128), buf(15, 8, 128), buf(4, 9, 8, 128),
        buf(4, 9, 8, 128),
        buf(8, 128), buf(4, 8, 128), buf(8, 128), buf(7, 8, 128),
        pltpu.SemaphoreType.DMA((64,)), pltpu.SemaphoreType.DMA((64,)), pltpu.SemaphoreType.DMA((4,)),
        pltpu.SemaphoreType.REGULAR,
    ]
    return pl.pallas_call(
        kernel,
        out_shape=(
            pltpu.VMEM(strain.shape, jnp.float32),
            pltpu.VMEM(velocity.shape, jnp.float32),
        ),
        in_specs=[hbm, hbm, hbm, hbm],
        out_specs=(vmem, vmem),
        scratch_shapes=scratch,
        compiler_params=pltpu.CompilerParams(
            collective_id=1, has_side_effects=True, vmem_limit_bytes=32 * 1024 * 1024),
        cost_estimate=pl.CostEstimate(flops=3_000_000, bytes_accessed=800_000, transcendentals=8192),
    )(*[pltpu.with_memory_space_constraint(v, pltpu.HBM) for v in (velocity, strain, row_bins, cotangent)])


def solution(mesh):
    field = P(None, "span", "stream", None)
    return jax.shard_map(
        on_device, mesh=mesh, in_specs=(field, field, P("stream"), field), out_specs=(field, field),
        check_vma=False)
```

```python
import jax
import jax.numpy as jnp
from jax import lax
from jax.experimental import pallas as pl
from jax.experimental.pallas import tpu as pltpu
from jax.sharding import PartitionSpec as P

ALPHA = 0.45
CENTER_WEIGHT = 0.95
SIDE_WEIGHT = 0.475
STRAIN_FLOOR = 0.25
EPSILON = 1e-06
PAIRS = ((0, 0), (0, 1), (0, 2), (1, 1), (1, 2), (2, 2))
WEIGHTS = (1.0, 2.0, 2.0, 1.0, 2.0, 1.0)
MESH = pl.DeviceIdType.MESH

ROOT = ((1.0 - 4.0 * ALPHA * ALPHA) ** 0.5 - 1.0) / (2.0 * ALPHA)
GREEN = 1.0 / (1.0 - 4.0 * ALPHA * ALPHA) ** 0.5
SCALE = SIDE_WEIGHT / ALPHA
REST = SCALE - CENTER_WEIGHT
OWN = SCALE + REST * GREEN
SWEEP = -REST * GREEN
CELLS, RING, GROUPS = 4, 4, 2
STEP = ROOT ** CELLS
AROUND = STEP ** RING
CLOSE = 1.0 / (1.0 - AROUND**GROUPS)
STREAM_STEPS = (-2, -1, 1, 2)


def ends(cells):
    right, left = cells[0], cells[3]
    for i in (1, 2, 3):
        right = cells[i] + ROOT * right
        left = cells[3 - i] + ROOT * left
    return right, left


def filtered_cells(cells, before, after):
    up, down = [], []
    for i in range(CELLS):
        before = cells[i] + ROOT * before
        after = cells[CELLS - 1 - i] + ROOT * after
        up.append(before)
        down.append(after)
    return [OWN * cells[i] + SWEEP * (up[i] + down[CELLS - 1 - i]) for i in range(CELLS)]


def carry(blocks):
    total = blocks[0]
    for p in (1, 2, 3):
        total = blocks[p] + STEP * total
    return total


def kernel(vel_in, strain_in, bins_in, cot_in, res, grad,
           vel, strain, bins, cot, fields, filt, leo, mod, back,
           e1, rb1, pa1, zb1, g1, ag1,
           ec, rbc, pac, zbc,
           e2, rb2, pa2, zb2, g2, ag2,
           t1, ts, t3, tz,
           send, recv, load, gate):
    span, stream = lax.axis_index("span"), lax.axis_index("stream")
    h, y = span // RING, lax.rem(span, RING)
    mirror = lax.rem(y, 2)
    place = y + mirror * (RING - 1 - 2 * y)

    def ring_peer(delta):
        return lax.rem(y + delta, RING)

    def ring_id(other):
        return (h * RING + other, stream)

    across = ((GROUPS - 1 - h) * RING + y, stream)

    def stream_id(step):
        turn = (lax.rem(stream, 16) + step + 16) // 16 - 1
        flip = turn * turn
        return ((h + flip - 2 * h * flip) * RING + y, lax.rem(stream + step + 64, 64))

    copies = []

    def push(src, dst, device):
        n = len(copies)
        copy = pltpu.make_async_remote_copy(
            src_ref=src, dst_ref=dst, send_sem=send.at[n], recv_sem=recv.at[n],
            device_id=device, device_id_type=MESH)
        copy.start()
        copies.append(copy)
        return copy

    def scatter(src, dst, at):
        out = []
        for delta in (2, 1, 3):
            other = ring_peer(delta)
            slot = y + lax.rem(other, 2) * (RING - 1 - 2 * y)
            out.append(push(src.at[other, at], dst.at[slot, at], ring_id(other)))
        dst[place, at] = src[y, at]
        return out

    def spread(src, dst, at):
        out = []
        for delta in (2, 1, 3):
            other = ring_peer(delta)
            slot = other + mirror * (RING - 1 - 2 * other)
            out.append(push(src.at[slot, at], dst.at[y, at], ring_id(other)))
        dst[y, at] = src[place, at]
        return out

    def arrive(group):
        for copy in group:
            copy.wait_recv()

    def keep_ends(buf, at, cells):
        right, left = ends(cells)
        for half in (0, 1):
            lanes = slice(128 * half, 128 * half + 128)
            buf[2 * half, at] = right[..., lanes]
            buf[2 * half + 1, at] = left[..., lanes]

    core = lax.rem(stream, 2)
    this_chip = stream - core

    def greet(sem, device):
        pl.semaphore_signal(sem, inc=1, device_id=device, device_id_type=MESH)

    def chip_id(step):
        there, position = stream_id(2 * step)
        return (there, position - core)

    barrier = pltpu.get_barrier_semaphore()
    greet(barrier, (across[0], this_chip))
    for d in (2, 1, 3):
        greet(barrier, (h * RING + ring_peer(d), this_chip + 1))
    greet(barrier, chip_id(-1))
    greet(barrier, chip_id(1))

    @pl.when(core == 0)
    def _():
        greet(barrier, (span, stream + 1))

    loads = [pltpu.make_async_copy(src, dst, load.at[n]) for n, (src, dst) in enumerate(
        ((vel_in, vel), (strain_in, strain), (cot_in, cot), (bins_in, bins)))]
    for one in loads:
        one.start()
    for one in loads:
        one.wait()

    for a in range(3):
        fields[a] = vel[a]
    total = jnp.zeros((CELLS, 8, 256), jnp.float32)
    for k, (a, b) in enumerate(PAIRS):
        fields[4 + k] = vel[a] * vel[b]
        total = total + WEIGHTS[k] * (strain[k] * strain[k])
    fields[3] = jnp.sqrt(jnp.maximum(2.0 * total, STRAIN_FLOOR))
    for f in range(10):
        keep_ends(e1, f, [fields[f, i] for i in range(CELLS)])
    row = lax.broadcasted_iota(jnp.int32, (8, 128), 0)
    lane = lax.broadcasted_iota(jnp.int32, (8, 128), 1)
    column = lax.rem(lane, 8)
    kind = lane // 8
    own_bins = jnp.zeros((8, 128), jnp.float32)
    lane_bins = jnp.zeros((8, 128), jnp.float32)
    for i in range(8):
        value = bins[i].astype(jnp.float32)
        own_bins = jnp.where(row == i, value, own_bins)
        lane_bins = jnp.where(column == i, value, lane_bins)

    def packed(three):
        wide = jnp.where(kind == 0, three[0], jnp.where(kind == 1, three[1], jnp.where(kind == 2, three[2], 0.0)))
        return jnp.sum(jnp.where(column == row, wide, 0.0), axis=0, keepdims=True)

    def columns_of(wide, mask):
        return [jnp.sum(jnp.where(mask & (kind == q), wide, 0.0), axis=-1, keepdims=True) for q in range(3)]

    @pl.when(core == 1)
    def _():
        pl.semaphore_wait(barrier, 2 * (RING - 1) + 1)
        greet(gate, (span, stream - 1))

    @pl.when(core == 0)
    def _():
        pl.semaphore_wait(gate, 1)

    early, late = slice(0, 4), slice(4, 10)
    scattered = [scatter(e1, rb1, at) for at in (early, late)]
    crossed, arrived = [], []
    for at, group in zip((early, late), scattered):
        arrive(group)
        pa1[at] = carry([rb1[p, at] for p in range(RING)])
        if not crossed:
            @pl.when(core == 0)
            def _():
                pl.semaphore_wait(barrier, 2 + 2 * 2)
                greet(gate, (span, stream + 1))

            @pl.when(core == 1)
            def _():
                pl.semaphore_wait(gate, 1)

        crossed.append(push(pa1.at[at], zb1.at[at], across))
    for k in range(6):
        keep_ends(ec, k, [cot[k, i] for i in range(CELLS)])
    first_cot = scatter(ec, rbc, slice(0, 6))
    for at, copy in zip((early, late), crossed):
        arrive([copy])
        entering = CLOSE * (zb1[at] + AROUND * pa1[at])
        g1[0, at] = entering
        for p in range(RING - 1):
            entering = rb1[p, at] + STEP * entering
            g1[p + 1, at] = entering
        arrived.append(spread(g1, ag1, at))
    arrive(arrived[0])
    for f in range(4):
        for half in (0, 1):
            lanes = slice(128 * half, 128 * half + 128)
            out = filtered_cells([fields[f, i, :, lanes] for i in range(CELLS)],
                                 ag1[2 * half, f], ag1[2 * half + 1, f])
            for i in range(CELLS):
                filt[f, i, :, lanes] = out[i]
    square = jnp.zeros((8, 256), jnp.float32)
    blame = jnp.zeros((8, 256), jnp.float32)
    for k, (a, b) in enumerate(PAIRS):
        weighted = []
        for i in range(CELLS):
            coarse = filt[a, i] * filt[b, i]
            model = fields[4 + k, i] - coarse + 2.0 * (4.0 * filt[3, i] - fields[3, i]) * strain[k, i]
            mod[k, i] = model
            weighted.append(WEIGHTS[k] * model)
            square = square + weighted[i] * model
            blame = blame + cot[k, i] * model
        keep_ends(e2, k, weighted)
    parts = (slice(0, 6), slice(6, 12), slice(12, 15))
    second = [scatter(e2, rb2, parts[0])]

    def with_filtered(a, slot, field):
        cells = []
        for i in range(CELLS):
            total = None
            for k, (former, latter) in enumerate(PAIRS):
                if a in (former, latter):
                    other = latter if former == a else former
                    term = field(k, i) * ((2.0 if former == latter else 1.0) * filt[other, i])
                    total = term if total is None else total + term
            back[slot, a, i] = total
            cells.append(total)
        keep_ends(e2, 6 + 3 * slot + a, cells)

    for a in range(3):
        with_filtered(a, 0, lambda k, i: cot[k, i])
        with_filtered(a, 1, lambda k, i: WEIGHTS[k] * mod[k, i])
    second.append(scatter(e2, rb2, parts[1]))

    arrive(first_cot)
    pac[...] = carry([rbc[p] for p in range(RING)])
    over_cot = push(pac, zbc, across)

    arrive(arrived[1])
    cross = jnp.zeros((8, 256), jnp.float32)
    for k, (a, b) in enumerate(PAIRS):
        halves = []
        for half in (0, 1):
            lanes = slice(128 * half, 128 * half + 128)
            halves.append(filtered_cells([fields[4 + k, i, :, lanes] for i in range(CELLS)],
                                         ag1[2 * half, 4 + k], ag1[2 * half + 1, 4 + k]))
        for i in range(CELLS):
            leonard = jnp.concatenate([halves[0][i], halves[1][i]], axis=-1) - filt[a, i] * filt[b, i]
            leo[k, i] = leonard
            cross = cross + WEIGHTS[k] * (leonard * mod[k, i])

    def over_lanes(values):
        return jnp.sum(values[:, :128] + values[:, 128:], axis=-1, keepdims=True)

    t1[0:1] = packed([over_lanes(cross), over_lanes(square), over_lanes(blame)])
    t1[1:2] = lane_bins[0:1]
    near = [push(t1, ts.at[n], stream_id(s)) for n, s in enumerate(STREAM_STEPS)]
    for a in range(3):
        with_filtered(a, 2, lambda k, i: WEIGHTS[k] * leo[k, i])
    second.append(scatter(e2, rb2, parts[2]))

    over2 = []

    def cross_part(n):
        at = parts[n]
        arrive(second[n])
        pa2[at] = carry([rb2[p, at] for p in range(RING)])
        over2.append(push(pa2.at[at], zb2.at[at], across))

    cross_part(0)
    arrive(near)
    wide = jnp.where(own_bins == t1[1:2], t1[0:1], 0.0)
    for n in range(4):
        wide = wide + jnp.where(own_bins == ts[n, 1:2], ts[n, 0:1], 0.0)
    t3[...] = packed(columns_of(wide, True))
    everywhere = [push(t3, tz.at[d - 1], (lax.rem(span + d, 8), stream)) for d in (4, 3, 5, 2, 6, 1, 7)]
    cross_part(1)
    cross_part(2)
    arrive(everywhere)
    total = t3[...]
    for d in range(7):
        total = total + tz[d]
    sums = columns_of(jnp.broadcast_to(total, (8, 128)), column == row)
    denominator = jnp.broadcast_to(sums[1], (8, 128)) + EPSILON
    coefficient = jnp.broadcast_to(sums[0], (8, 128)) / denominator
    row_cross = -jnp.broadcast_to(sums[2], (8, 128)) / denominator
    row_square = -2.0 * row_cross * coefficient
    row_model = row_cross + row_square
    spare = coefficient - 1.0

    def adjoint(at, blocks, other):
        entering = CLOSE * (other + AROUND * carry(blocks))
        g2[0, at] = entering
        for p in range(RING - 1):
            entering = blocks[p] + STEP * entering
            g2[p + 1, at] = entering
        return spread(g2, ag2, at)

    def coarse_part(buf, *p):
        return (spare * buf[(*p, slice(6, 9))] - row_model * buf[(*p, slice(9, 12))]
                - row_cross * buf[(*p, slice(12, 15))])

    arrive([over_cot, over2[0]])
    last = adjoint(slice(3, 9), [rbc[p] + row_cross * rb2[p, 0:6] for p in range(RING)],
                   zbc[...] + row_cross * zb2[0:6])
    arrive(over2[1:])
    last = last + adjoint(slice(0, 3), [coarse_part(rb2, p) for p in range(RING)], coarse_part(zb2))

    def wide(values):
        return jnp.concatenate([values, values], axis=-1)

    coefficient, row_cross, row_square, row_model, spare = (
        wide(coefficient), wide(row_cross), wide(row_square), wide(row_model), wide(spare))
    for a in range(3):
        for i in range(CELLS):
            back[0, a, i] = spare * back[0, a, i] - row_model * back[1, a, i] - row_cross * back[2, a, i]
    for k in range(6):
        for i in range(CELLS):
            leonard, model, bar = leo[k, i], mod[k, i], cot[k, i]
            res[k, i] = leonard - coefficient * model
            weighted = WEIGHTS[k] * row_cross
            leo[k, i] = bar + weighted * model
            mod[k, i] = weighted * leonard - coefficient * bar + (WEIGHTS[k] * row_square) * model
    arrive(last)
    for half in (0, 1):
        lanes = slice(128 * half, 128 * half + 128)
        sums = []
        for a in range(3):
            sums.append(filtered_cells([back[0, a, i, :, lanes] for i in range(CELLS)],
                                       ag2[2 * half, a], ag2[2 * half + 1, a]))
        for k, (a, b) in enumerate(PAIRS):
            pulled = filtered_cells([leo[k, i, :, lanes] for i in range(CELLS)],
                                    ag2[2 * half, 3 + k], ag2[2 * half + 1, 3 + k])
            for i in range(CELLS):
                through = pulled[i] + mod[k, i, :, lanes]
                sums[a][i] = sums[a][i] + through * vel[b, i, :, lanes]
                sums[b][i] = sums[b][i] + through * vel[a, i, :, lanes]
        for a in range(3):
            for i in range(CELLS):
                grad[a, i, :, lanes] = sums[a][i]
    for copy in copies:
        copy.wait_send()


def on_device(velocity, strain, row_bins, cotangent):
    def buf(*shape):
        return pltpu.VMEM(shape, jnp.float32)

    vmem = pl.BlockSpec(memory_space=pltpu.VMEM)
    hbm = pl.BlockSpec(memory_space=pltpu.HBM)
    scratch = [
        buf(3, 4, 8, 256), buf(6, 4, 8, 256), pltpu.SMEM((8,), jnp.int32), buf(6, 4, 8, 256),
        buf(10, 4, 8, 256), buf(4, 4, 8, 256), buf(6, 4, 8, 256), buf(6, 4, 8, 256), buf(3, 3, 4, 8, 256),
        buf(4, 10, 8, 128), buf(4, 10, 8, 128), buf(10, 8, 128), buf(10, 8, 128), buf(4, 10, 8, 128),
        buf(4, 10, 8, 128),
        buf(4, 6, 8, 128), buf(4, 6, 8, 128), buf(6, 8, 128), buf(6, 8, 128),
        buf(4, 15, 8, 128), buf(4, 15, 8, 128), buf(15, 8, 128), buf(15, 8, 128), buf(4, 9, 8, 128),
        buf(4, 9, 8, 128),
        buf(2, 128), buf(4, 2, 128), buf(1, 128), buf(7, 1, 128),
        pltpu.SemaphoreType.DMA((64,)), pltpu.SemaphoreType.DMA((64,)), pltpu.SemaphoreType.DMA((4,)),
        pltpu.SemaphoreType.REGULAR,
    ]
    return pl.pallas_call(
        kernel,
        out_shape=(
            pltpu.VMEM(strain.shape, jnp.float32),
            pltpu.VMEM(velocity.shape, jnp.float32),
        ),
        in_specs=[hbm, hbm, hbm, hbm],
        out_specs=(vmem, vmem),
        scratch_shapes=scratch,
        compiler_params=pltpu.CompilerParams(
            collective_id=1, has_side_effects=True, vmem_limit_bytes=32 * 1024 * 1024),
        cost_estimate=pl.CostEstimate(flops=3_000_000, bytes_accessed=800_000, transcendentals=8192),
    )(*[pltpu.with_memory_space_constraint(v, pltpu.HBM) for v in (velocity, strain, row_bins, cotangent)])


def solution(mesh):
    field = P(None, "span", "stream", None)
    return jax.shard_map(
        on_device, mesh=mesh, in_specs=(field, field, P("stream"), field), out_specs=(field, field),
        check_vma=False)
```

```python
import jax
import jax.numpy as jnp
from jax import lax
from jax.experimental import pallas as pl
from jax.experimental.pallas import tpu as pltpu
from jax.sharding import PartitionSpec as P

ALPHA = 0.45
CENTER_WEIGHT = 0.95
SIDE_WEIGHT = 0.475
STRAIN_FLOOR = 0.25
EPSILON = 1e-06
PAIRS = ((0, 0), (0, 1), (0, 2), (1, 1), (1, 2), (2, 2))
WEIGHTS = (1.0, 2.0, 2.0, 1.0, 2.0, 1.0)
MESH = pl.DeviceIdType.MESH

ROOT = ((1.0 - 4.0 * ALPHA * ALPHA) ** 0.5 - 1.0) / (2.0 * ALPHA)
GREEN = 1.0 / (1.0 - 4.0 * ALPHA * ALPHA) ** 0.5
SCALE = SIDE_WEIGHT / ALPHA
REST = SCALE - CENTER_WEIGHT
OWN = SCALE + REST * GREEN
SWEEP = -REST * GREEN
CELLS, RING, GROUPS = 4, 4, 2
STEP = ROOT ** CELLS
AROUND = STEP ** RING
CLOSE = 1.0 / (1.0 - AROUND**GROUPS)
STREAM_STEPS = (-2, -1, 1, 2)


def ends(cells):
    right, left = cells[0], cells[3]
    for i in (1, 2, 3):
        right = cells[i] + ROOT * right
        left = cells[3 - i] + ROOT * left
    return right, left


def filtered_cells(cells, before, after):
    up, down = [], []
    for i in range(CELLS):
        before = cells[i] + ROOT * before
        after = cells[CELLS - 1 - i] + ROOT * after
        up.append(before)
        down.append(after)
    return [OWN * cells[i] + SWEEP * (up[i] + down[CELLS - 1 - i]) for i in range(CELLS)]


def carry(blocks):
    total = blocks[0]
    for p in (1, 2, 3):
        total = blocks[p] + STEP * total
    return total


def kernel(vel_in, strain_in, bins_in, cot_in, res, grad,
           vel, strain, bins, cot, fields, filt, leo, mod, back,
           e1, rb1, pa1, zb1, g1, ag1,
           ec, rbc, pac, zbc,
           e2, rb2, pa2, zb2, g2, ag2,
           t1, ts, t3, tz,
           send, recv, load, gate):
    span, stream = lax.axis_index("span"), lax.axis_index("stream")
    h, y = span // RING, lax.rem(span, RING)
    mirror = lax.rem(y, 2)
    place = y + mirror * (RING - 1 - 2 * y)

    def ring_peer(delta):
        return lax.rem(y + delta, RING)

    def ring_id(other):
        return (h * RING + other, stream)

    across = ((GROUPS - 1 - h) * RING + y, stream)

    def stream_id(step):
        turn = (lax.rem(stream, 16) + step + 16) // 16 - 1
        flip = turn * turn
        return ((h + flip - 2 * h * flip) * RING + y, lax.rem(stream + step + 64, 64))

    copies = []

    def push(src, dst, device):
        n = len(copies)
        copy = pltpu.make_async_remote_copy(
            src_ref=src, dst_ref=dst, send_sem=send.at[n], recv_sem=recv.at[n],
            device_id=device, device_id_type=MESH)
        copy.start()
        copies.append(copy)
        return copy

    def scatter(src, dst, at):
        out = []
        for delta in (2, 1, 3):
            other = ring_peer(delta)
            slot = y + lax.rem(other, 2) * (RING - 1 - 2 * y)
            out.append(push(src.at[other, at], dst.at[slot, at], ring_id(other)))
        dst[place, at] = src[y, at]
        return out

    def spread(src, dst, at):
        out = []
        for delta in (2, 1, 3):
            other = ring_peer(delta)
            slot = other + mirror * (RING - 1 - 2 * other)
            out.append(push(src.at[slot, at], dst.at[y, at], ring_id(other)))
        dst[y, at] = src[place, at]
        return out

    def arrive(group):
        for copy in group:
            copy.wait_recv()

    def keep_ends(buf, at, cells):
        right, left = ends(cells)
        for half in (0, 1):
            lanes = slice(128 * half, 128 * half + 128)
            buf[2 * half, at] = right[..., lanes]
            buf[2 * half + 1, at] = left[..., lanes]

    core = lax.rem(stream, 2)
    this_chip = stream - core

    def greet(sem, device):
        pl.semaphore_signal(sem, inc=1, device_id=device, device_id_type=MESH)

    def chip_id(step):
        there, position = stream_id(2 * step)
        return (there, position - core)

    barrier = pltpu.get_barrier_semaphore()
    greet(barrier, (across[0], this_chip))
    for d in (2, 1, 3):
        greet(barrier, (h * RING + ring_peer(d), this_chip + 1))
    greet(barrier, chip_id(-1))
    greet(barrier, chip_id(1))

    @pl.when(core == 0)
    def _():
        greet(barrier, (span, stream + 1))

    loads = [pltpu.make_async_copy(src, dst, load.at[n]) for n, (src, dst) in enumerate(
        ((vel_in, vel), (strain_in, strain), (cot_in, cot), (bins_in, bins)))]
    for one in loads:
        one.start()
    for one in loads:
        one.wait()

    for a in range(3):
        fields[a] = vel[a]
    total = jnp.zeros((CELLS, 8, 256), jnp.float32)
    for k, (a, b) in enumerate(PAIRS):
        fields[4 + k] = vel[a] * vel[b]
        total = total + WEIGHTS[k] * (strain[k] * strain[k])
    fields[3] = jnp.sqrt(jnp.maximum(2.0 * total, STRAIN_FLOOR))
    for f in range(10):
        keep_ends(e1, f, [fields[f, i] for i in range(CELLS)])
    row = lax.broadcasted_iota(jnp.int32, (8, 128), 0)
    lane = lax.broadcasted_iota(jnp.int32, (8, 128), 1)
    column = lax.rem(lane, 8)
    kind = lane // 8
    own_bins = jnp.zeros((8, 128), jnp.float32)
    lane_bins = jnp.zeros((8, 128), jnp.float32)
    for i in range(8):
        value = bins[i].astype(jnp.float32)
        own_bins = jnp.where(row == i, value, own_bins)
        lane_bins = jnp.where(column == i, value, lane_bins)

    def packed(three):
        wide = jnp.where(kind == 0, three[0], jnp.where(kind == 1, three[1], jnp.where(kind == 2, three[2], 0.0)))
        return jnp.sum(jnp.where(column == row, wide, 0.0), axis=0, keepdims=True)

    def columns_of(wide, mask):
        return [jnp.sum(jnp.where(mask & (kind == q), wide, 0.0), axis=-1, keepdims=True) for q in range(3)]

    @pl.when(core == 1)
    def _():
        pl.semaphore_wait(barrier, 2 * (RING - 1) + 1)
        greet(gate, (span, stream - 1))

    @pl.when(core == 0)
    def _():
        pl.semaphore_wait(gate, 1)

    early, late = slice(0, 4), slice(4, 10)
    scattered = [scatter(e1, rb1, at) for at in (early, late)]
    crossed, arrived = [], []
    for at, group in zip((early, late), scattered):
        arrive(group)
        pa1[at] = carry([rb1[p, at] for p in range(RING)])
        if not crossed:
            @pl.when(core == 0)
            def _():
                pl.semaphore_wait(barrier, 2 + 2 * 2)
                greet(gate, (span, stream + 1))

            @pl.when(core == 1)
            def _():
                pl.semaphore_wait(gate, 1)

        crossed.append(push(pa1.at[at], zb1.at[at], across))
    for k in range(6):
        keep_ends(ec, k, [cot[k, i] for i in range(CELLS)])
    first_cot = scatter(ec, rbc, slice(0, 6))
    for at, copy in zip((early, late), crossed):
        arrive([copy])
        entering = CLOSE * (zb1[at] + AROUND * pa1[at])
        g1[0, at] = entering
        for p in range(RING - 1):
            entering = rb1[p, at] + STEP * entering
            g1[p + 1, at] = entering
        arrived.append(spread(g1, ag1, at))
    arrive(arrived[0])
    for f in range(4):
        for half in (0, 1):
            lanes = slice(128 * half, 128 * half + 128)
            out = filtered_cells([fields[f, i, :, lanes] for i in range(CELLS)],
                                 ag1[2 * half, f], ag1[2 * half + 1, f])
            for i in range(CELLS):
                filt[f, i, :, lanes] = out[i]
    square = jnp.zeros((8, 256), jnp.float32)
    blame = jnp.zeros((8, 256), jnp.float32)
    for k, (a, b) in enumerate(PAIRS):
        weighted = []
        for i in range(CELLS):
            coarse = filt[a, i] * filt[b, i]
            model = fields[4 + k, i] - coarse + 2.0 * (4.0 * filt[3, i] - fields[3, i]) * strain[k, i]
            mod[k, i] = model
            weighted.append(WEIGHTS[k] * model)
            square = square + weighted[i] * model
            blame = blame + cot[k, i] * model
        keep_ends(e2, k, weighted)
    parts = (slice(0, 6), slice(6, 12), slice(12, 15))
    second = [scatter(e2, rb2, parts[0])]

    def with_filtered(a, slot, field):
        cells = []
        for i in range(CELLS):
            total = None
            for k, (former, latter) in enumerate(PAIRS):
                if a in (former, latter):
                    other = latter if former == a else former
                    term = field(k, i) * ((2.0 if former == latter else 1.0) * filt[other, i])
                    total = term if total is None else total + term
            back[slot, a, i] = total
            cells.append(total)
        keep_ends(e2, 6 + 3 * slot + a, cells)

    for a in range(3):
        with_filtered(a, 0, lambda k, i: cot[k, i])
        with_filtered(a, 1, lambda k, i: WEIGHTS[k] * mod[k, i])
    second.append(scatter(e2, rb2, parts[1]))

    arrive(first_cot)
    pac[...] = carry([rbc[p] for p in range(RING)])
    over_cot = push(pac, zbc, across)

    arrive(arrived[1])
    cross = jnp.zeros((8, 256), jnp.float32)
    for k, (a, b) in enumerate(PAIRS):
        halves = []
        for half in (0, 1):
            lanes = slice(128 * half, 128 * half + 128)
            halves.append(filtered_cells([fields[4 + k, i, :, lanes] for i in range(CELLS)],
                                         ag1[2 * half, 4 + k], ag1[2 * half + 1, 4 + k]))
        for i in range(CELLS):
            leonard = jnp.concatenate([halves[0][i], halves[1][i]], axis=-1) - filt[a, i] * filt[b, i]
            leo[k, i] = leonard
            cross = cross + WEIGHTS[k] * (leonard * mod[k, i])

    def over_lanes(values):
        return jnp.sum(values[:, :128] + values[:, 128:], axis=-1, keepdims=True)

    t1[0:1] = packed([over_lanes(cross), over_lanes(square), over_lanes(blame)])
    t1[1:2] = lane_bins[0:1]
    near = [push(t1, ts.at[n], stream_id(s)) for n, s in enumerate(STREAM_STEPS)]
    for a in range(3):
        with_filtered(a, 2, lambda k, i: WEIGHTS[k] * leo[k, i])
    second.append(scatter(e2, rb2, parts[2]))

    over2 = []

    def cross_part(n):
        at = parts[n]
        arrive(second[n])
        pa2[at] = carry([rb2[p, at] for p in range(RING)])
        over2.append(push(pa2.at[at], zb2.at[at], across))

    cross_part(0)
    arrive(near)
    wide = jnp.where(own_bins == t1[1:2], t1[0:1], 0.0)
    for n in range(4):
        wide = wide + jnp.where(own_bins == ts[n, 1:2], ts[n, 0:1], 0.0)
    t3[...] = packed(columns_of(wide, True))
    everywhere = [push(t3, tz.at[d - 1], (lax.rem(span + d, 8), stream)) for d in (4, 3, 5, 2, 6, 1, 7)]
    cross_part(1)
    cross_part(2)
    arrive(everywhere)
    total = t3[...]
    for d in range(7):
        total = total + tz[d]
    sums = columns_of(jnp.broadcast_to(total, (8, 128)), column == row)
    denominator = jnp.broadcast_to(sums[1], (8, 128)) + EPSILON
    coefficient = jnp.broadcast_to(sums[0], (8, 128)) / denominator
    row_cross = -jnp.broadcast_to(sums[2], (8, 128)) / denominator
    row_square = -2.0 * row_cross * coefficient
    row_model = row_cross + row_square
    spare = coefficient - 1.0

    def adjoint(at, blocks, other):
        entering = CLOSE * (other + AROUND * carry(blocks))
        g2[0, at] = entering
        for p in range(RING - 1):
            entering = blocks[p] + STEP * entering
            g2[p + 1, at] = entering
        return spread(g2, ag2, at)

    def coarse_part(buf, *p):
        return (spare * buf[(*p, slice(6, 9))] - row_model * buf[(*p, slice(9, 12))]
                - row_cross * buf[(*p, slice(12, 15))])

    arrive([over_cot, over2[0]])
    last = adjoint(slice(3, 9), [rbc[p] + row_cross * rb2[p, 0:6] for p in range(RING)],
                   zbc[...] + row_cross * zb2[0:6])
    arrive(over2[1:])
    last = last + adjoint(slice(0, 3), [coarse_part(rb2, p) for p in range(RING)], coarse_part(zb2))

    def wide(values):
        return jnp.concatenate([values, values], axis=-1)

    coefficient, row_cross, row_square, row_model, spare = (
        wide(coefficient), wide(row_cross), wide(row_square), wide(row_model), wide(spare))
    for a in range(3):
        for i in range(CELLS):
            back[0, a, i] = spare * back[0, a, i] - row_model * back[1, a, i] - row_cross * back[2, a, i]
    for k in range(6):
        for i in range(CELLS):
            leonard, model, bar = leo[k, i], mod[k, i], cot[k, i]
            res[k, i] = leonard - coefficient * model
            weighted = WEIGHTS[k] * row_cross
            leo[k, i] = bar + weighted * model
            mod[k, i] = weighted * leonard - coefficient * bar + (WEIGHTS[k] * row_square) * model
    arrive(last)
    for half in (0, 1):
        lanes = slice(128 * half, 128 * half + 128)
        sums = []
        for a in range(3):
            sums.append(filtered_cells([back[0, a, i, :, lanes] for i in range(CELLS)],
                                       ag2[2 * half, a], ag2[2 * half + 1, a]))
        for k, (a, b) in enumerate(PAIRS):
            pulled = filtered_cells([leo[k, i, :, lanes] for i in range(CELLS)],
                                    ag2[2 * half, 3 + k], ag2[2 * half + 1, 3 + k])
            for i in range(CELLS):
                through = pulled[i] + mod[k, i, :, lanes]
                sums[a][i] = sums[a][i] + through * vel[b, i, :, lanes]
                sums[b][i] = sums[b][i] + through * vel[a, i, :, lanes]
        for a in range(3):
            for i in range(CELLS):
                grad[a, i, :, lanes] = sums[a][i]
    for copy in copies:
        copy.wait_send()


def store_both(first, second, first_out, second_out, done):
    copies = [pltpu.make_async_copy(first, first_out, done.at[0]), pltpu.make_async_copy(second, second_out, done.at[1])]
    for copy in copies:
        copy.start()
    for copy in copies:
        copy.wait()


def on_device(velocity, strain, row_bins, cotangent):
    def buf(*shape):
        return pltpu.VMEM(shape, jnp.float32)

    vmem = pl.BlockSpec(memory_space=pltpu.VMEM)
    hbm = pl.BlockSpec(memory_space=pltpu.HBM)
    scratch = [
        buf(3, 4, 8, 256), buf(6, 4, 8, 256), pltpu.SMEM((8,), jnp.int32), buf(6, 4, 8, 256),
        buf(10, 4, 8, 256), buf(4, 4, 8, 256), buf(6, 4, 8, 256), buf(6, 4, 8, 256), buf(3, 3, 4, 8, 256),
        buf(4, 10, 8, 128), buf(4, 10, 8, 128), buf(10, 8, 128), buf(10, 8, 128), buf(4, 10, 8, 128),
        buf(4, 10, 8, 128),
        buf(4, 6, 8, 128), buf(4, 6, 8, 128), buf(6, 8, 128), buf(6, 8, 128),
        buf(4, 15, 8, 128), buf(4, 15, 8, 128), buf(15, 8, 128), buf(15, 8, 128), buf(4, 9, 8, 128),
        buf(4, 9, 8, 128),
        buf(2, 128), buf(4, 2, 128), buf(1, 128), buf(7, 1, 128),
        pltpu.SemaphoreType.DMA((64,)), pltpu.SemaphoreType.DMA((64,)), pltpu.SemaphoreType.DMA((4,)),
        pltpu.SemaphoreType.REGULAR,
    ]
    results = pl.pallas_call(
        kernel,
        out_shape=(
            pltpu.VMEM(strain.shape, jnp.float32),
            pltpu.VMEM(velocity.shape, jnp.float32),
        ),
        in_specs=[hbm, hbm, hbm, hbm],
        out_specs=(vmem, vmem),
        scratch_shapes=scratch,
        compiler_params=pltpu.CompilerParams(
            collective_id=1, has_side_effects=True, vmem_limit_bytes=32 * 1024 * 1024),
        cost_estimate=pl.CostEstimate(flops=3_000_000, bytes_accessed=800_000, transcendentals=8192),
    )(*[pltpu.with_memory_space_constraint(v, pltpu.HBM) for v in (velocity, strain, row_bins, cotangent)])
    return pl.pallas_call(
        store_both,
        out_shape=(pltpu.HBM(strain.shape, jnp.float32), pltpu.HBM(velocity.shape, jnp.float32)),
        in_specs=[vmem, vmem],
        out_specs=(hbm, hbm),
        scratch_shapes=[pltpu.SemaphoreType.DMA((2,))],
    )(*[pltpu.with_memory_space_constraint(v, pltpu.VMEM) for v in results])


def solution(mesh):
    field = P(None, "span", "stream", None)
    return jax.shard_map(
        on_device, mesh=mesh, in_specs=(field, field, P("stream"), field), out_specs=(field, field),
        check_vma=False)
```

```python
import jax
import jax.numpy as jnp
from jax import lax
from jax.experimental import pallas as pl
from jax.experimental.pallas import tpu as pltpu
from jax.sharding import PartitionSpec as P

ALPHA = 0.45
CENTER_WEIGHT = 0.95
SIDE_WEIGHT = 0.475
STRAIN_FLOOR = 0.25
EPSILON = 1e-06
PAIRS = ((0, 0), (0, 1), (0, 2), (1, 1), (1, 2), (2, 2))
WEIGHTS = (1.0, 2.0, 2.0, 1.0, 2.0, 1.0)
MESH = pl.DeviceIdType.MESH

ROOT = ((1.0 - 4.0 * ALPHA * ALPHA) ** 0.5 - 1.0) / (2.0 * ALPHA)
GREEN = 1.0 / (1.0 - 4.0 * ALPHA * ALPHA) ** 0.5
SCALE = SIDE_WEIGHT / ALPHA
REST = SCALE - CENTER_WEIGHT
OWN = SCALE + REST * GREEN
SWEEP = -REST * GREEN
CELLS, RING, GROUPS = 4, 4, 2
STEP = ROOT ** CELLS
AROUND = STEP ** RING
CLOSE = 1.0 / (1.0 - AROUND**GROUPS)
STREAM_STEPS = (-2, -1, 1, 2)


def ends(cells):
    right, left = cells[0], cells[3]
    for i in (1, 2, 3):
        right = cells[i] + ROOT * right
        left = cells[3 - i] + ROOT * left
    return right, left


def filtered_cells(cells, before, after):
    up, down = [], []
    for i in range(CELLS):
        before = cells[i] + ROOT * before
        after = cells[CELLS - 1 - i] + ROOT * after
        up.append(before)
        down.append(after)
    return [OWN * cells[i] + SWEEP * (up[i] + down[CELLS - 1 - i]) for i in range(CELLS)]


def carry(blocks):
    total = blocks[0]
    for p in (1, 2, 3):
        total = blocks[p] + STEP * total
    return total


def kernel(vel_in, strain_in, bins_in, cot_in, res, grad,
           vel, strain, bins, cot, fields, filt, leo, mod, back,
           e1, rb1, pa1, zb1, g1, ag1,
           ec, rbc, pac, zbc,
           e2, rb2, pa2, zb2, g2, ag2,
           t0, ts, t1, tz,
           send, recv, load, gate):
    span, stream = lax.axis_index("span"), lax.axis_index("stream")
    h, y = span // RING, lax.rem(span, RING)
    mirror = lax.rem(y, 2)
    place = y + mirror * (RING - 1 - 2 * y)

    def ring_peer(delta):
        return lax.rem(y + delta, RING)

    def ring_id(other):
        return (h * RING + other, stream)

    across = ((GROUPS - 1 - h) * RING + y, stream)

    def stream_id(step):
        turn = (lax.rem(stream, 16) + step + 16) // 16 - 1
        flip = turn * turn
        return ((h + flip - 2 * h * flip) * RING + y, lax.rem(stream + step + 64, 64))

    copies = []

    def push(src, dst, device):
        n = len(copies)
        copy = pltpu.make_async_remote_copy(
            src_ref=src, dst_ref=dst, send_sem=send.at[n], recv_sem=recv.at[n],
            device_id=device, device_id_type=MESH)
        copy.start()
        copies.append(copy)
        return copy

    def scatter(src, dst, at):
        out = []
        for delta in (2, 1, 3):
            other = ring_peer(delta)
            slot = y + lax.rem(other, 2) * (RING - 1 - 2 * y)
            out.append(push(src.at[other, at], dst.at[slot, at], ring_id(other)))
        dst[place, at] = src[y, at]
        return out

    def spread(src, dst, at):
        out = []
        for delta in (2, 1, 3):
            other = ring_peer(delta)
            slot = other + mirror * (RING - 1 - 2 * other)
            out.append(push(src.at[slot, at], dst.at[y, at], ring_id(other)))
        dst[y, at] = src[place, at]
        return out

    def arrive(group):
        for copy in group:
            copy.wait_recv()

    def keep_ends(buf, at, cells):
        right, left = ends(cells)
        for half in (0, 1):
            lanes = slice(128 * half, 128 * half + 128)
            buf[2 * half, at] = right[..., lanes]
            buf[2 * half + 1, at] = left[..., lanes]

    core = lax.rem(stream, 2)
    this_chip = stream - core

    def greet(sem, device):
        pl.semaphore_signal(sem, inc=1, device_id=device, device_id_type=MESH)

    def chip_id(step):
        there, position = stream_id(2 * step)
        return (there, position - core)

    barrier = pltpu.get_barrier_semaphore()
    greet(barrier, (across[0], this_chip))
    for d in (2, 1, 3):
        greet(barrier, (h * RING + ring_peer(d), this_chip + 1))
    greet(barrier, chip_id(-1))
    greet(barrier, chip_id(1))

    @pl.when(core == 0)
    def _():
        greet(barrier, (span, stream + 1))

    loads = [pltpu.make_async_copy(src, dst, load.at[n]) for n, (src, dst) in enumerate(
        ((vel_in, vel), (strain_in, strain), (cot_in, cot), (bins_in, bins)))]
    for one in loads:
        one.start()
    for one in loads:
        one.wait()

    for a in range(3):
        fields[a] = vel[a]
    total = jnp.zeros((CELLS, 8, 256), jnp.float32)
    for k, (a, b) in enumerate(PAIRS):
        fields[4 + k] = vel[a] * vel[b]
        total = total + WEIGHTS[k] * (strain[k] * strain[k])
    fields[3] = jnp.sqrt(jnp.maximum(2.0 * total, STRAIN_FLOOR))
    for f in range(10):
        keep_ends(e1, f, [fields[f, i] for i in range(CELLS)])
    row = lax.broadcasted_iota(jnp.int32, (8, 128), 0)
    lane = lax.broadcasted_iota(jnp.int32, (8, 128), 1)
    column = lax.rem(lane, 8)
    kind = lane // 8
    own_bins = jnp.zeros((8, 128), jnp.float32)
    lane_bins = jnp.zeros((8, 128), jnp.float32)
    for i in range(8):
        value = bins[i].astype(jnp.float32)
        own_bins = jnp.where(row == i, value, own_bins)
        lane_bins = jnp.where(column == i, value, lane_bins)

    t0[...] = lane_bins[0:1]

    def packed(three):
        wide = jnp.where(kind == 0, three[0], jnp.where(kind == 1, three[1], jnp.where(kind == 2, three[2], 0.0)))
        return jnp.sum(jnp.where(column == row, wide, 0.0), axis=0, keepdims=True)

    @pl.when(core == 1)
    def _():
        pl.semaphore_wait(barrier, 2 * (RING - 1) + 1)
        greet(gate, (span, stream - 1))

    @pl.when(core == 0)
    def _():
        pl.semaphore_wait(gate, 1)

    early, late = slice(0, 4), slice(4, 10)
    scattered = [scatter(e1, rb1, at) for at in (early, late)]
    crossed, arrived = [], []
    for at, group in zip((early, late), scattered):
        arrive(group)
        pa1[at] = carry([rb1[p, at] for p in range(RING)])
        if not crossed:
            @pl.when(core == 0)
            def _():
                pl.semaphore_wait(barrier, 2 + 2 * 2)
                greet(gate, (span, stream + 1))

            @pl.when(core == 1)
            def _():
                pl.semaphore_wait(gate, 1)

        crossed.append(push(pa1.at[at], zb1.at[at], across))
    for k in range(6):
        keep_ends(ec, k, [cot[k, i] for i in range(CELLS)])
    first_cot = scatter(ec, rbc, slice(0, 6))
    near_bins = [push(t0, ts.at[n], stream_id(s)) for n, s in enumerate(STREAM_STEPS)]
    for at, copy in zip((early, late), crossed):
        arrive([copy])
        entering = CLOSE * (zb1[at] + AROUND * pa1[at])
        g1[0, at] = entering
        for p in range(RING - 1):
            entering = rb1[p, at] + STEP * entering
            g1[p + 1, at] = entering
        arrived.append(spread(g1, ag1, at))
    arrive(arrived[0])
    for f in range(4):
        for half in (0, 1):
            lanes = slice(128 * half, 128 * half + 128)
            out = filtered_cells([fields[f, i, :, lanes] for i in range(CELLS)],
                                 ag1[2 * half, f], ag1[2 * half + 1, f])
            for i in range(CELLS):
                filt[f, i, :, lanes] = out[i]
    square = jnp.zeros((8, 256), jnp.float32)
    blame = jnp.zeros((8, 256), jnp.float32)
    for k, (a, b) in enumerate(PAIRS):
        weighted = []
        for i in range(CELLS):
            coarse = filt[a, i] * filt[b, i]
            model = fields[4 + k, i] - coarse + 2.0 * (4.0 * filt[3, i] - fields[3, i]) * strain[k, i]
            mod[k, i] = model
            weighted.append(WEIGHTS[k] * model)
            square = square + weighted[i] * model
            blame = blame + cot[k, i] * model
        keep_ends(e2, k, weighted)
    parts = (slice(0, 6), slice(6, 12), slice(12, 15))
    second = [scatter(e2, rb2, parts[0])]

    def with_filtered(a, slot, field):
        cells = []
        for i in range(CELLS):
            total = None
            for k, (former, latter) in enumerate(PAIRS):
                if a in (former, latter):
                    other = latter if former == a else former
                    term = field(k, i) * ((2.0 if former == latter else 1.0) * filt[other, i])
                    total = term if total is None else total + term
            back[slot, a, i] = total
            cells.append(total)
        keep_ends(e2, 6 + 3 * slot + a, cells)

    for a in range(3):
        with_filtered(a, 0, lambda k, i: cot[k, i])
        with_filtered(a, 1, lambda k, i: WEIGHTS[k] * mod[k, i])
    second.append(scatter(e2, rb2, parts[1]))

    arrive(first_cot)
    pac[...] = carry([rbc[p] for p in range(RING)])
    over_cot = push(pac, zbc, across)

    arrive(arrived[1])
    cross = jnp.zeros((8, 256), jnp.float32)
    for k, (a, b) in enumerate(PAIRS):
        halves = []
        for half in (0, 1):
            lanes = slice(128 * half, 128 * half + 128)
            halves.append(filtered_cells([fields[4 + k, i, :, lanes] for i in range(CELLS)],
                                         ag1[2 * half, 4 + k], ag1[2 * half + 1, 4 + k]))
        for i in range(CELLS):
            leonard = jnp.concatenate([halves[0][i], halves[1][i]], axis=-1) - filt[a, i] * filt[b, i]
            leo[k, i] = leonard
            cross = cross + WEIGHTS[k] * (leonard * mod[k, i])

    def over_lanes(values):
        return jnp.sum(values[:, :128] + values[:, 128:], axis=-1, keepdims=True)

    t1[...] = packed([over_lanes(cross), over_lanes(square), over_lanes(blame)])
    everywhere = []
    for far, turn in ((1, 0), (1, 1), (1, 3), (1, 2), (0, 2), (0, 1), (0, 3), (0, 0)):
        there = (h + far - 2 * h * far) * RING + ring_peer(turn)
        for n, step in enumerate(STREAM_STEPS + (0,)):
            if (far, turn, step) != (0, 0, 0):
                everywhere.append(push(t1, tz.at[n, 4 * far + turn], (there, lax.rem(stream + step + 64, 64))))
    tz[4, 0] = t1[...]
    for a in range(3):
        with_filtered(a, 2, lambda k, i: WEIGHTS[k] * leo[k, i])
    second.append(scatter(e2, rb2, parts[2]))

    over2 = []

    def cross_part(n):
        at = parts[n]
        arrive(second[n])
        pa2[at] = carry([rb2[p, at] for p in range(RING)])
        over2.append(push(pa2.at[at], zb2.at[at], across))

    cross_part(0)
    cross_part(1)
    cross_part(2)
    arrive(near_bins)
    arrive(everywhere)
    wide = jnp.zeros((8, 128), jnp.float32)
    for n in range(5):
        total = tz[n, 0]
        for slot in range(1, 8):
            total = total + tz[n, slot]
        wide = wide + jnp.where(own_bins == (ts[n] if n < 4 else t0[...]), total, 0.0)
    sums = [jnp.sum(jnp.where(kind == q, wide, 0.0), axis=-1, keepdims=True) for q in range(3)]
    denominator = jnp.broadcast_to(sums[1], (8, 128)) + EPSILON
    coefficient = jnp.broadcast_to(sums[0], (8, 128)) / denominator
    row_cross = -jnp.broadcast_to(sums[2], (8, 128)) / denominator
    row_square = -2.0 * row_cross * coefficient
    row_model = row_cross + row_square
    spare = coefficient - 1.0

    def adjoint(at, blocks, other):
        entering = CLOSE * (other + AROUND * carry(blocks))
        g2[0, at] = entering
        for p in range(RING - 1):
            entering = blocks[p] + STEP * entering
            g2[p + 1, at] = entering
        return spread(g2, ag2, at)

    def coarse_part(buf, *p):
        return (spare * buf[(*p, slice(6, 9))] - row_model * buf[(*p, slice(9, 12))]
                - row_cross * buf[(*p, slice(12, 15))])

    arrive([over_cot, over2[0]])
    last = adjoint(slice(3, 9), [rbc[p] + row_cross * rb2[p, 0:6] for p in range(RING)],
                   zbc[...] + row_cross * zb2[0:6])
    arrive(over2[1:])
    last = last + adjoint(slice(0, 3), [coarse_part(rb2, p) for p in range(RING)], coarse_part(zb2))

    def wide(values):
        return jnp.concatenate([values, values], axis=-1)

    coefficient, row_cross, row_square, row_model, spare = (
        wide(coefficient), wide(row_cross), wide(row_square), wide(row_model), wide(spare))
    for a in range(3):
        for i in range(CELLS):
            back[0, a, i] = spare * back[0, a, i] - row_model * back[1, a, i] - row_cross * back[2, a, i]
    for k in range(6):
        for i in range(CELLS):
            leonard, model, bar = leo[k, i], mod[k, i], cot[k, i]
            res[k, i] = leonard - coefficient * model
            weighted = WEIGHTS[k] * row_cross
            leo[k, i] = bar + weighted * model
            mod[k, i] = weighted * leonard - coefficient * bar + (WEIGHTS[k] * row_square) * model
    for copy in copies[:-6]:
        copy.wait_send()
    arrive(last)
    for half in (0, 1):
        lanes = slice(128 * half, 128 * half + 128)
        sums = []
        for a in range(3):
            sums.append(filtered_cells([back[0, a, i, :, lanes] for i in range(CELLS)],
                                       ag2[2 * half, a], ag2[2 * half + 1, a]))
        for k, (a, b) in enumerate(PAIRS):
            pulled = filtered_cells([leo[k, i, :, lanes] for i in range(CELLS)],
                                    ag2[2 * half, 3 + k], ag2[2 * half + 1, 3 + k])
            for i in range(CELLS):
                through = pulled[i] + mod[k, i, :, lanes]
                sums[a][i] = sums[a][i] + through * vel[b, i, :, lanes]
                sums[b][i] = sums[b][i] + through * vel[a, i, :, lanes]
        for a in range(3):
            for i in range(CELLS):
                grad[a, i, :, lanes] = sums[a][i]
    for copy in copies[-6:]:
        copy.wait_send()


def store_both(first, second, first_out, second_out, done):
    copies = [pltpu.make_async_copy(first, first_out, done.at[0]), pltpu.make_async_copy(second, second_out, done.at[1])]
    for copy in copies:
        copy.start()
    for copy in copies:
        copy.wait()


def on_device(velocity, strain, row_bins, cotangent):
    def buf(*shape):
        return pltpu.VMEM(shape, jnp.float32)

    vmem = pl.BlockSpec(memory_space=pltpu.VMEM)
    hbm = pl.BlockSpec(memory_space=pltpu.HBM)
    scratch = [
        buf(3, 4, 8, 256), buf(6, 4, 8, 256), pltpu.SMEM((8,), jnp.int32), buf(6, 4, 8, 256),
        buf(10, 4, 8, 256), buf(4, 4, 8, 256), buf(6, 4, 8, 256), buf(6, 4, 8, 256), buf(3, 3, 4, 8, 256),
        buf(4, 10, 8, 128), buf(4, 10, 8, 128), buf(10, 8, 128), buf(10, 8, 128), buf(4, 10, 8, 128),
        buf(4, 10, 8, 128),
        buf(4, 6, 8, 128), buf(4, 6, 8, 128), buf(6, 8, 128), buf(6, 8, 128),
        buf(4, 15, 8, 128), buf(4, 15, 8, 128), buf(15, 8, 128), buf(15, 8, 128), buf(4, 9, 8, 128),
        buf(4, 9, 8, 128),
        buf(1, 128), buf(4, 1, 128), buf(1, 128), buf(5, 8, 1, 128),
        pltpu.SemaphoreType.DMA((96,)), pltpu.SemaphoreType.DMA((96,)), pltpu.SemaphoreType.DMA((4,)),
        pltpu.SemaphoreType.REGULAR,
    ]
    results = pl.pallas_call(
        kernel,
        out_shape=(
            pltpu.VMEM(strain.shape, jnp.float32),
            pltpu.VMEM(velocity.shape, jnp.float32),
        ),
        in_specs=[hbm, hbm, hbm, hbm],
        out_specs=(vmem, vmem),
        scratch_shapes=scratch,
        compiler_params=pltpu.CompilerParams(
            collective_id=1, has_side_effects=True, vmem_limit_bytes=32 * 1024 * 1024),
        cost_estimate=pl.CostEstimate(flops=3_000_000, bytes_accessed=800_000, transcendentals=8192),
    )(*[pltpu.with_memory_space_constraint(v, pltpu.HBM) for v in (velocity, strain, row_bins, cotangent)])
    return pl.pallas_call(
        store_both,
        out_shape=(pltpu.HBM(strain.shape, jnp.float32), pltpu.HBM(velocity.shape, jnp.float32)),
        in_specs=[vmem, vmem],
        out_specs=(hbm, hbm),
        scratch_shapes=[pltpu.SemaphoreType.DMA((2,))],
    )(*[pltpu.with_memory_space_constraint(v, pltpu.VMEM) for v in results])


def solution(mesh):
    field = P(None, "span", "stream", None)
    return jax.shard_map(
        on_device, mesh=mesh, in_specs=(field, field, P("stream"), field), out_specs=(field, field),
        check_vma=False)
```

```python
import jax
import jax.numpy as jnp
from jax import lax
from jax.experimental import pallas as pl
from jax.experimental.pallas import tpu as pltpu
from jax.sharding import PartitionSpec as P

ALPHA = 0.45
CENTER_WEIGHT = 0.95
SIDE_WEIGHT = 0.475
STRAIN_FLOOR = 0.25
EPSILON = 1e-06
PAIRS = ((0, 0), (0, 1), (0, 2), (1, 1), (1, 2), (2, 2))
WEIGHTS = (1.0, 2.0, 2.0, 1.0, 2.0, 1.0)
MESH = pl.DeviceIdType.MESH

ROOT = ((1.0 - 4.0 * ALPHA * ALPHA) ** 0.5 - 1.0) / (2.0 * ALPHA)
GREEN = 1.0 / (1.0 - 4.0 * ALPHA * ALPHA) ** 0.5
SCALE = SIDE_WEIGHT / ALPHA
REST = SCALE - CENTER_WEIGHT
OWN = SCALE + REST * GREEN
SWEEP = -REST * GREEN
CELLS, RING, GROUPS = 4, 4, 2
STEP = ROOT ** CELLS
AROUND = STEP ** RING
CLOSE = 1.0 / (1.0 - AROUND**GROUPS)
STREAM_STEPS = (-2, -1, 1, 2)


def ends(cells):
    right, left = cells[0], cells[3]
    for i in (1, 2, 3):
        right = cells[i] + ROOT * right
        left = cells[3 - i] + ROOT * left
    return right, left


def filtered_cells(cells, before, after):
    up, down = [], []
    for i in range(CELLS):
        before = cells[i] + ROOT * before
        after = cells[CELLS - 1 - i] + ROOT * after
        up.append(before)
        down.append(after)
    return [OWN * cells[i] + SWEEP * (up[i] + down[CELLS - 1 - i]) for i in range(CELLS)]


def carry(blocks):
    total = blocks[0]
    for p in (1, 2, 3):
        total = blocks[p] + STEP * total
    return total


def kernel(vel_in, strain_in, bins_in, cot_in, res, grad,
           vel, strain, bins, cot, fields, filt, leo, mod, back,
           e1, rb1, pa1, zb1, g1, ag1,
           ec, rbc, pac, zbc,
           e2, rb2, pa2, zb2, g2, ag2,
           t0, ts, t1, tz,
           send, recv, load, gate):
    span, stream = lax.axis_index("span"), lax.axis_index("stream")
    h, y = span // RING, lax.rem(span, RING)
    mirror = lax.rem(y, 2)
    place = y + mirror * (RING - 1 - 2 * y)

    def ring_peer(delta):
        return lax.rem(y + delta, RING)

    def ring_id(other):
        return (h * RING + other, stream)

    across = ((GROUPS - 1 - h) * RING + y, stream)

    def stream_id(step):
        turn = (lax.rem(stream, 16) + step + 16) // 16 - 1
        flip = turn * turn
        return ((h + flip - 2 * h * flip) * RING + y, lax.rem(stream + step + 64, 64))

    copies = []

    def push(src, dst, device):
        n = len(copies)
        copy = pltpu.make_async_remote_copy(
            src_ref=src, dst_ref=dst, send_sem=send.at[n], recv_sem=recv.at[n],
            device_id=device, device_id_type=MESH)
        copy.start()
        copies.append(copy)
        return copy

    def scatter(src, dst, at):
        out = []
        for delta in (2, 1, 3):
            other = ring_peer(delta)
            slot = y + lax.rem(other, 2) * (RING - 1 - 2 * y)
            out.append(push(src.at[other, at], dst.at[slot, at], ring_id(other)))
        dst[place, at] = src[y, at]
        return out

    def spread(src, dst, at):
        out = []
        for delta in (2, 1, 3):
            other = ring_peer(delta)
            slot = other + mirror * (RING - 1 - 2 * other)
            out.append(push(src.at[slot, at], dst.at[y, at], ring_id(other)))
        dst[y, at] = src[place, at]
        return out

    def arrive(group):
        for copy in group:
            copy.wait_recv()

    def keep_ends(buf, at, cells):
        right, left = ends(cells)
        for half in (0, 1):
            lanes = slice(128 * half, 128 * half + 128)
            buf[2 * half, at] = right[..., lanes]
            buf[2 * half + 1, at] = left[..., lanes]

    core = lax.rem(stream, 2)
    this_chip = stream - core

    def greet(sem, device):
        pl.semaphore_signal(sem, inc=1, device_id=device, device_id_type=MESH)

    def chip_id(step):
        there, position = stream_id(2 * step)
        return (there, position - core)

    barrier = pltpu.get_barrier_semaphore()
    greet(barrier, (across[0], this_chip))
    for d in (2, 1, 3):
        greet(barrier, (h * RING + ring_peer(d), this_chip + 1))
    greet(barrier, chip_id(-1))
    greet(barrier, chip_id(1))

    @pl.when(core == 0)
    def _():
        greet(barrier, (span, stream + 1))

    loads = [pltpu.make_async_copy(src, dst, load.at[n]) for n, (src, dst) in enumerate(
        ((vel_in, vel), (strain_in, strain), (cot_in, cot), (bins_in, bins)))]
    for one in loads:
        one.start()
    loads[0].wait()
    loads[1].wait()

    for a in range(3):
        fields[a] = vel[a]
    total = jnp.zeros((CELLS, 8, 256), jnp.float32)
    for k, (a, b) in enumerate(PAIRS):
        fields[4 + k] = vel[a] * vel[b]
        total = total + WEIGHTS[k] * (strain[k] * strain[k])
    fields[3] = jnp.sqrt(jnp.maximum(2.0 * total, STRAIN_FLOOR))
    for f in range(10):
        keep_ends(e1, f, [fields[f, i] for i in range(CELLS)])
    @pl.when(core == 1)
    def _():
        pl.semaphore_wait(barrier, 2 * (RING - 1) + 1)
        greet(gate, (span, stream - 1))

    @pl.when(core == 0)
    def _():
        pl.semaphore_wait(gate, 1)

    early, late = slice(0, 4), slice(4, 10)
    scattered = [scatter(e1, rb1, at) for at in (early, late)]
    loads[2].wait()
    loads[3].wait()
    row = lax.broadcasted_iota(jnp.int32, (8, 128), 0)
    lane = lax.broadcasted_iota(jnp.int32, (8, 128), 1)
    column = lax.rem(lane, 8)
    kind = lane // 8
    own_bins = jnp.zeros((8, 128), jnp.float32)
    lane_bins = jnp.zeros((8, 128), jnp.float32)
    for i in range(8):
        value = bins[i].astype(jnp.float32)
        own_bins = jnp.where(row == i, value, own_bins)
        lane_bins = jnp.where(column == i, value, lane_bins)

    t0[...] = lane_bins[0:1]

    def packed(three):
        wide = jnp.where(kind == 0, three[0], jnp.where(kind == 1, three[1], jnp.where(kind == 2, three[2], 0.0)))
        return jnp.sum(jnp.where(column == row, wide, 0.0), axis=0, keepdims=True)

    crossed, arrived = [], []
    for at, group in zip((early, late), scattered):
        arrive(group)
        pa1[at] = carry([rb1[p, at] for p in range(RING)])
        if not crossed:
            @pl.when(core == 0)
            def _():
                pl.semaphore_wait(barrier, 2 + 2 * 2)
                greet(gate, (span, stream + 1))

            @pl.when(core == 1)
            def _():
                pl.semaphore_wait(gate, 1)

        crossed.append(push(pa1.at[at], zb1.at[at], across))
    for k in range(6):
        keep_ends(ec, k, [cot[k, i] for i in range(CELLS)])
    first_cot = scatter(ec, rbc, slice(0, 6))
    near_bins = [push(t0, ts.at[n], stream_id(s)) for n, s in enumerate(STREAM_STEPS)]
    for at, copy in zip((early, late), crossed):
        arrive([copy])
        entering = CLOSE * (zb1[at] + AROUND * pa1[at])
        g1[0, at] = entering
        for p in range(RING - 1):
            entering = rb1[p, at] + STEP * entering
            g1[p + 1, at] = entering
        arrived.append(spread(g1, ag1, at))
        if len(arrived) == 1:
            arrive(first_cot)
            pac[...] = carry([rbc[p] for p in range(RING)])
            over_cot = push(pac, zbc, across)
    arrive(arrived[0])
    for f in range(4):
        for half in (0, 1):
            lanes = slice(128 * half, 128 * half + 128)
            out = filtered_cells([fields[f, i, :, lanes] for i in range(CELLS)],
                                 ag1[2 * half, f], ag1[2 * half + 1, f])
            for i in range(CELLS):
                filt[f, i, :, lanes] = out[i]
    square = jnp.zeros((8, 256), jnp.float32)
    blame = jnp.zeros((8, 256), jnp.float32)
    for k, (a, b) in enumerate(PAIRS):
        weighted = []
        for i in range(CELLS):
            coarse = filt[a, i] * filt[b, i]
            model = fields[4 + k, i] - coarse + 2.0 * (4.0 * filt[3, i] - fields[3, i]) * strain[k, i]
            mod[k, i] = model
            weighted.append(WEIGHTS[k] * model)
            square = square + weighted[i] * model
            blame = blame + cot[k, i] * model
        keep_ends(e2, k, weighted)
    parts = (slice(0, 6), slice(6, 12), slice(12, 15))
    second = [scatter(e2, rb2, parts[0])]

    def with_filtered(a, slot, field):
        cells = []
        for i in range(CELLS):
            total = None
            for k, (former, latter) in enumerate(PAIRS):
                if a in (former, latter):
                    other = latter if former == a else former
                    term = field(k, i) * ((2.0 if former == latter else 1.0) * filt[other, i])
                    total = term if total is None else total + term
            back[slot, a, i] = total
            cells.append(total)
        keep_ends(e2, 6 + 3 * slot + a, cells)

    for a in range(3):
        with_filtered(a, 0, lambda k, i: cot[k, i])
        with_filtered(a, 1, lambda k, i: WEIGHTS[k] * mod[k, i])
    second.append(scatter(e2, rb2, parts[1]))

    arrive(arrived[1])
    cross = jnp.zeros((8, 256), jnp.float32)
    for k, (a, b) in enumerate(PAIRS):
        halves = []
        for half in (0, 1):
            lanes = slice(128 * half, 128 * half + 128)
            halves.append(filtered_cells([fields[4 + k, i, :, lanes] for i in range(CELLS)],
                                         ag1[2 * half, 4 + k], ag1[2 * half + 1, 4 + k]))
        for i in range(CELLS):
            leonard = jnp.concatenate([halves[0][i], halves[1][i]], axis=-1) - filt[a, i] * filt[b, i]
            leo[k, i] = leonard
            cross = cross + WEIGHTS[k] * (leonard * mod[k, i])

    def over_lanes(values):
        return jnp.sum(values[:, :128] + values[:, 128:], axis=-1, keepdims=True)

    t1[...] = packed([over_lanes(cross), over_lanes(square), over_lanes(blame)])
    everywhere = []

    def tell(far, turns):
        there = h + far - 2 * h * far
        for turn in turns:
            for n, step in enumerate(STREAM_STEPS + (0,)):
                if (far, turn, step) != (0, 0, 0):
                    everywhere.append(push(t1, tz.at[n, 4 * far + turn],
                                           (there * RING + ring_peer(turn), lax.rem(stream + step + 64, 64))))

    tell(1, (2, 1, 3, 0))
    tz[4, 0] = t1[...]
    for a in range(3):
        with_filtered(a, 2, lambda k, i: WEIGHTS[k] * leo[k, i])
    second.append(scatter(e2, rb2, parts[2]))

    over2 = []

    def cross_part(n):
        at = parts[n]
        arrive(second[n])
        pa2[at] = carry([rb2[p, at] for p in range(RING)])
        over2.append(push(pa2.at[at], zb2.at[at], across))

    tell(0, (2, 1, 3, 0))
    cross_part(0)
    cross_part(1)
    cross_part(2)
    arrive(near_bins)
    arrive(everywhere)
    wide = jnp.zeros((8, 128), jnp.float32)
    for n in range(5):
        total = tz[n, 0]
        for slot in range(1, 8):
            total = total + tz[n, slot]
        wide = wide + jnp.where(own_bins == (ts[n] if n < 4 else t0[...]), total, 0.0)
    sums = [jnp.sum(jnp.where(kind == q, wide, 0.0), axis=-1, keepdims=True) for q in range(3)]
    denominator = jnp.broadcast_to(sums[1], (8, 128)) + EPSILON
    coefficient = jnp.broadcast_to(sums[0], (8, 128)) / denominator
    row_cross = -jnp.broadcast_to(sums[2], (8, 128)) / denominator
    row_square = -2.0 * row_cross * coefficient
    row_model = row_cross + row_square
    spare = coefficient - 1.0

    def adjoint(at, blocks, other):
        entering = CLOSE * (other + AROUND * carry(blocks))
        g2[0, at] = entering
        for p in range(RING - 1):
            entering = blocks[p] + STEP * entering
            g2[p + 1, at] = entering
        return spread(g2, ag2, at)

    def coarse_part(buf, *p):
        return (spare * buf[(*p, slice(6, 9))] - row_model * buf[(*p, slice(9, 12))]
                - row_cross * buf[(*p, slice(12, 15))])

    arrive([over_cot, over2[0]])
    last = adjoint(slice(3, 9), [rbc[p] + row_cross * rb2[p, 0:6] for p in range(RING)],
                   zbc[...] + row_cross * zb2[0:6])
    arrive(over2[1:])
    last = last + adjoint(slice(0, 3), [coarse_part(rb2, p) for p in range(RING)], coarse_part(zb2))

    def wide(values):
        return jnp.concatenate([values, values], axis=-1)

    coefficient, row_cross, row_square, row_model, spare = (
        wide(coefficient), wide(row_cross), wide(row_square), wide(row_model), wide(spare))
    for a in range(3):
        for i in range(CELLS):
            back[0, a, i] = spare * back[0, a, i] - row_model * back[1, a, i] - row_cross * back[2, a, i]
    for k in range(6):
        for i in range(CELLS):
            leonard, model, bar = leo[k, i], mod[k, i], cot[k, i]
            res[k, i] = leonard - coefficient * model
            weighted = WEIGHTS[k] * row_cross
            leo[k, i] = bar + weighted * model
            mod[k, i] = weighted * leonard - coefficient * bar + (WEIGHTS[k] * row_square) * model
    for copy in copies[:-6]:
        copy.wait_send()
    arrive(last)
    for half in (0, 1):
        lanes = slice(128 * half, 128 * half + 128)
        sums = []
        for a in range(3):
            sums.append(filtered_cells([back[0, a, i, :, lanes] for i in range(CELLS)],
                                       ag2[2 * half, a], ag2[2 * half + 1, a]))
        for k, (a, b) in enumerate(PAIRS):
            pulled = filtered_cells([leo[k, i, :, lanes] for i in range(CELLS)],
                                    ag2[2 * half, 3 + k], ag2[2 * half + 1, 3 + k])
            for i in range(CELLS):
                through = pulled[i] + mod[k, i, :, lanes]
                sums[a][i] = sums[a][i] + through * vel[b, i, :, lanes]
                sums[b][i] = sums[b][i] + through * vel[a, i, :, lanes]
        for a in range(3):
            for i in range(CELLS):
                grad[a, i, :, lanes] = sums[a][i]
    for copy in copies[-6:]:
        copy.wait_send()


def store_both(first, second, first_out, second_out, done):
    copies = [pltpu.make_async_copy(first, first_out, done.at[0]), pltpu.make_async_copy(second, second_out, done.at[1])]
    for copy in copies:
        copy.start()
    for copy in copies:
        copy.wait()


def on_device(velocity, strain, row_bins, cotangent):
    def buf(*shape):
        return pltpu.VMEM(shape, jnp.float32)

    vmem = pl.BlockSpec(memory_space=pltpu.VMEM)
    hbm = pl.BlockSpec(memory_space=pltpu.HBM)
    scratch = [
        buf(3, 4, 8, 256), buf(6, 4, 8, 256), pltpu.SMEM((8,), jnp.int32), buf(6, 4, 8, 256),
        buf(10, 4, 8, 256), buf(4, 4, 8, 256), buf(6, 4, 8, 256), buf(6, 4, 8, 256), buf(3, 3, 4, 8, 256),
        buf(4, 10, 8, 128), buf(4, 10, 8, 128), buf(10, 8, 128), buf(10, 8, 128), buf(4, 10, 8, 128),
        buf(4, 10, 8, 128),
        buf(4, 6, 8, 128), buf(4, 6, 8, 128), buf(6, 8, 128), buf(6, 8, 128),
        buf(4, 15, 8, 128), buf(4, 15, 8, 128), buf(15, 8, 128), buf(15, 8, 128), buf(4, 9, 8, 128),
        buf(4, 9, 8, 128),
        buf(1, 128), buf(4, 1, 128), buf(1, 128), buf(5, 8, 1, 128),
        pltpu.SemaphoreType.DMA((96,)), pltpu.SemaphoreType.DMA((96,)), pltpu.SemaphoreType.DMA((4,)),
        pltpu.SemaphoreType.REGULAR,
    ]
    results = pl.pallas_call(
        kernel,
        out_shape=(
            pltpu.VMEM(strain.shape, jnp.float32),
            pltpu.VMEM(velocity.shape, jnp.float32),
        ),
        in_specs=[hbm, hbm, hbm, hbm],
        out_specs=(vmem, vmem),
        scratch_shapes=scratch,
        compiler_params=pltpu.CompilerParams(
            collective_id=1, has_side_effects=True, vmem_limit_bytes=32 * 1024 * 1024),
        cost_estimate=pl.CostEstimate(flops=3_000_000, bytes_accessed=800_000, transcendentals=8192),
    )(*[pltpu.with_memory_space_constraint(v, pltpu.HBM) for v in (velocity, strain, row_bins, cotangent)])
    return pl.pallas_call(
        store_both,
        out_shape=(pltpu.HBM(strain.shape, jnp.float32), pltpu.HBM(velocity.shape, jnp.float32)),
        in_specs=[vmem, vmem],
        out_specs=(hbm, hbm),
        scratch_shapes=[pltpu.SemaphoreType.DMA((2,))],
    )(*[pltpu.with_memory_space_constraint(v, pltpu.VMEM) for v in results])


def solution(mesh):
    field = P(None, "span", "stream", None)
    return jax.shard_map(
        on_device, mesh=mesh, in_specs=(field, field, P("stream"), field), out_specs=(field, field),
        check_vma=False)
```

```python
import jax
import jax.numpy as jnp
from jax import lax
from jax.experimental import pallas as pl
from jax.experimental.pallas import tpu as pltpu
from jax.sharding import PartitionSpec as P

ALPHA = 0.45
CENTER_WEIGHT = 0.95
SIDE_WEIGHT = 0.475
STRAIN_FLOOR = 0.25
EPSILON = 1e-06
PAIRS = ((0, 0), (0, 1), (0, 2), (1, 1), (1, 2), (2, 2))
WEIGHTS = (1.0, 2.0, 2.0, 1.0, 2.0, 1.0)
MESH = pl.DeviceIdType.MESH

ROOT = ((1.0 - 4.0 * ALPHA * ALPHA) ** 0.5 - 1.0) / (2.0 * ALPHA)
GREEN = 1.0 / (1.0 - 4.0 * ALPHA * ALPHA) ** 0.5
SCALE = SIDE_WEIGHT / ALPHA
REST = SCALE - CENTER_WEIGHT
OWN = SCALE + REST * GREEN
SWEEP = -REST * GREEN
CELLS, RING, GROUPS = 4, 4, 2
STEP = ROOT ** CELLS
AROUND = STEP ** RING
CLOSE = 1.0 / (1.0 - AROUND**GROUPS)
STREAM_STEPS = (-2, -1, 1, 2)


def ends(cells):
    right, left = cells[0], cells[3]
    for i in (1, 2, 3):
        right = cells[i] + ROOT * right
        left = cells[3 - i] + ROOT * left
    return right, left


def filtered_cells(cells, before, after):
    up, down = [], []
    for i in range(CELLS):
        before = cells[i] + ROOT * before
        after = cells[CELLS - 1 - i] + ROOT * after
        up.append(before)
        down.append(after)
    return [OWN * cells[i] + SWEEP * (up[i] + down[CELLS - 1 - i]) for i in range(CELLS)]


def carry(blocks):
    total = blocks[0]
    for p in (1, 2, 3):
        total = blocks[p] + STEP * total
    return total


def kernel(vel_in, strain_in, bins_in, cot_in, res, grad,
           vel, strain, bins, cot, fields, filt, leo, mod, back,
           e1, rb1, pa1, zb1, g1, ag1,
           ec, rbc, pac, zbc,
           e2, rb2, pa2, zb2, g2, ag2,
           t0, ts, t1, tz,
           send, recv, load, gate):
    span, stream = lax.axis_index("span"), lax.axis_index("stream")
    h, y = span // RING, lax.rem(span, RING)
    mirror = lax.rem(y, 2)
    place = y + mirror * (RING - 1 - 2 * y)

    def ring_peer(delta):
        return lax.rem(y + delta, RING)

    def ring_id(other):
        return (h * RING + other, stream)

    across = ((GROUPS - 1 - h) * RING + y, stream)

    def stream_id(step):
        turn = (lax.rem(stream, 16) + step + 16) // 16 - 1
        flip = turn * turn
        return ((h + flip - 2 * h * flip) * RING + y, lax.rem(stream + step + 64, 64))

    copies = []

    def push(src, dst, device):
        n = len(copies)
        copy = pltpu.make_async_remote_copy(
            src_ref=src, dst_ref=dst, send_sem=send.at[n], recv_sem=recv.at[n],
            device_id=device, device_id_type=MESH)
        copy.start()
        copies.append(copy)
        return copy

    def scatter(src, dst, at):
        out = []
        for delta in (2, 1, 3):
            other = ring_peer(delta)
            slot = y + lax.rem(other, 2) * (RING - 1 - 2 * y)
            out.append(push(src.at[other, at], dst.at[slot, at], ring_id(other)))
        dst[place, at] = src[y, at]
        return out

    def spread(src, dst, at):
        out = []
        for delta in (2, 1, 3):
            other = ring_peer(delta)
            slot = other + mirror * (RING - 1 - 2 * other)
            out.append(push(src.at[slot, at], dst.at[y, at], ring_id(other)))
        dst[y, at] = src[place, at]
        return out

    def arrive(group):
        for copy in group:
            copy.wait_recv()

    def keep_ends(buf, at, cells):
        right, left = ends(cells)
        for half in (0, 1):
            lanes = slice(128 * half, 128 * half + 128)
            buf[2 * half, at] = right[..., lanes]
            buf[2 * half + 1, at] = left[..., lanes]

    core = lax.rem(stream, 2)
    this_chip = stream - core

    def greet(sem, device):
        pl.semaphore_signal(sem, inc=1, device_id=device, device_id_type=MESH)

    def chip_id(step):
        there, position = stream_id(2 * step)
        return (there, position - core + 1)

    barrier = pltpu.get_barrier_semaphore()
    greet(barrier, (across[0], this_chip + 1))
    for d in (2, 1, 3):
        greet(barrier, (h * RING + ring_peer(d), this_chip))
    greet(barrier, chip_id(-1))
    greet(barrier, chip_id(1))

    @pl.when(core == 1)
    def _():
        greet(barrier, (span, stream - 1))

    loads = [pltpu.make_async_copy(src, dst, load.at[n]) for n, (src, dst) in enumerate(
        ((vel_in, vel), (strain_in, strain), (cot_in, cot), (bins_in, bins)))]
    for one in loads:
        one.start()
    loads[0].wait()
    loads[1].wait()

    for a in range(3):
        fields[a] = vel[a]
    total = jnp.zeros((CELLS, 8, 256), jnp.float32)
    for k, (a, b) in enumerate(PAIRS):
        fields[4 + k] = vel[a] * vel[b]
        total = total + WEIGHTS[k] * (strain[k] * strain[k])
    fields[3] = jnp.sqrt(jnp.maximum(2.0 * total, STRAIN_FLOOR))
    for f in range(10):
        keep_ends(e1, f, [fields[f, i] for i in range(CELLS)])
    @pl.when(core == 0)
    def _():
        pl.semaphore_wait(barrier, 2 * (RING - 1) + 1)
        greet(gate, (span, stream + 1))

    @pl.when(core == 1)
    def _():
        pl.semaphore_wait(gate, 1)

    early, late = slice(0, 4), slice(4, 10)
    scattered = [scatter(e1, rb1, at) for at in (early, late)]
    loads[2].wait()
    loads[3].wait()
    row = lax.broadcasted_iota(jnp.int32, (8, 128), 0)
    lane = lax.broadcasted_iota(jnp.int32, (8, 128), 1)
    column = lax.rem(lane, 8)
    kind = lane // 8
    own_bins = jnp.zeros((8, 128), jnp.float32)
    lane_bins = jnp.zeros((8, 128), jnp.float32)
    for i in range(8):
        value = bins[i].astype(jnp.float32)
        own_bins = jnp.where(row == i, value, own_bins)
        lane_bins = jnp.where(column == i, value, lane_bins)

    t0[...] = lane_bins[0:1]

    def packed(three):
        wide = jnp.where(kind == 0, three[0], jnp.where(kind == 1, three[1], jnp.where(kind == 2, three[2], 0.0)))
        return jnp.sum(jnp.where(column == row, wide, 0.0), axis=0, keepdims=True)

    crossed, arrived = [], []
    for at, group in zip((early, late), scattered):
        arrive(group)
        pa1[at] = carry([rb1[p, at] for p in range(RING)])
        if not crossed:
            @pl.when(core == 1)
            def _():
                pl.semaphore_wait(barrier, 2 + 2 * 2)
                greet(gate, (span, stream - 1))

            @pl.when(core == 0)
            def _():
                pl.semaphore_wait(gate, 1)

        crossed.append(push(pa1.at[at], zb1.at[at], across))
    for k in range(6):
        keep_ends(ec, k, [cot[k, i] for i in range(CELLS)])
    first_cot = scatter(ec, rbc, slice(0, 6))
    near_bins = [push(t0, ts.at[n], stream_id(s)) for n, s in enumerate(STREAM_STEPS)]
    for at, copy in zip((early, late), crossed):
        arrive([copy])
        entering = CLOSE * (zb1[at] + AROUND * pa1[at])
        g1[0, at] = entering
        for p in range(RING - 1):
            entering = rb1[p, at] + STEP * entering
            g1[p + 1, at] = entering
        arrived.append(spread(g1, ag1, at))
        if len(arrived) == 1:
            arrive(first_cot)
            pac[...] = carry([rbc[p] for p in range(RING)])
            over_cot = push(pac, zbc, across)
    arrive(arrived[0])
    for f in range(4):
        for half in (0, 1):
            lanes = slice(128 * half, 128 * half + 128)
            out = filtered_cells([fields[f, i, :, lanes] for i in range(CELLS)],
                                 ag1[2 * half, f], ag1[2 * half + 1, f])
            for i in range(CELLS):
                filt[f, i, :, lanes] = out[i]
    square = jnp.zeros((8, 256), jnp.float32)
    blame = jnp.zeros((8, 256), jnp.float32)
    for k, (a, b) in enumerate(PAIRS):
        weighted = []
        for i in range(CELLS):
            coarse = filt[a, i] * filt[b, i]
            model = fields[4 + k, i] - coarse + 2.0 * (4.0 * filt[3, i] - fields[3, i]) * strain[k, i]
            mod[k, i] = model
            weighted.append(WEIGHTS[k] * model)
            square = square + weighted[i] * model
            blame = blame + cot[k, i] * model
        keep_ends(e2, k, weighted)
    parts = (slice(0, 3), slice(3, 6), slice(6, 12), slice(12, 15))
    second = [scatter(e2, rb2, parts[0]), scatter(e2, rb2, parts[1])]

    def with_filtered(a, slot, field):
        cells = []
        for i in range(CELLS):
            total = None
            for k, (former, latter) in enumerate(PAIRS):
                if a in (former, latter):
                    other = latter if former == a else former
                    term = field(k, i) * ((2.0 if former == latter else 1.0) * filt[other, i])
                    total = term if total is None else total + term
            back[slot, a, i] = total
            cells.append(total)
        keep_ends(e2, 6 + 3 * slot + a, cells)

    for a in range(3):
        with_filtered(a, 0, lambda k, i: cot[k, i])
        with_filtered(a, 1, lambda k, i: WEIGHTS[k] * mod[k, i])
    second.append(scatter(e2, rb2, parts[2]))

    arrive(arrived[1])
    cross = jnp.zeros((8, 256), jnp.float32)
    for k, (a, b) in enumerate(PAIRS):
        halves = []
        for half in (0, 1):
            lanes = slice(128 * half, 128 * half + 128)
            halves.append(filtered_cells([fields[4 + k, i, :, lanes] for i in range(CELLS)],
                                         ag1[2 * half, 4 + k], ag1[2 * half + 1, 4 + k]))
        for i in range(CELLS):
            leonard = jnp.concatenate([halves[0][i], halves[1][i]], axis=-1) - filt[a, i] * filt[b, i]
            leo[k, i] = leonard
            cross = cross + WEIGHTS[k] * (leonard * mod[k, i])

    def over_lanes(values):
        return jnp.sum(values[:, :128] + values[:, 128:], axis=-1, keepdims=True)

    t1[...] = packed([over_lanes(cross), over_lanes(square), over_lanes(blame)])
    everywhere = []

    def tell(far, turns):
        there = h + far - 2 * h * far
        for turn in turns:
            for n, step in enumerate(STREAM_STEPS + (0,)):
                if (far, turn, step) != (0, 0, 0):
                    everywhere.append(push(t1, tz.at[n, 4 * far + turn],
                                           (there * RING + ring_peer(turn), lax.rem(stream + step + 64, 64))))

    tell(1, (2, 1, 3, 0))
    tz[4, 0] = t1[...]
    for a in range(3):
        with_filtered(a, 2, lambda k, i: WEIGHTS[k] * leo[k, i])
    second.append(scatter(e2, rb2, parts[3]))

    over2 = []

    def cross_part(n):
        at = parts[n]
        arrive(second[n])
        pa2[at] = carry([rb2[p, at] for p in range(RING)])
        over2.append(push(pa2.at[at], zb2.at[at], across))

    tell(0, (2, 1, 3, 0))
    cross_part(0)
    cross_part(1)
    cross_part(2)
    cross_part(3)
    arrive(near_bins)
    arrive(everywhere)
    wide = jnp.zeros((8, 128), jnp.float32)
    for n in range(5):
        total = tz[n, 0]
        for slot in range(1, 8):
            total = total + tz[n, slot]
        wide = wide + jnp.where(own_bins == (ts[n] if n < 4 else t0[...]), total, 0.0)
    sums = [jnp.sum(jnp.where(kind == q, wide, 0.0), axis=-1, keepdims=True) for q in range(3)]
    denominator = jnp.broadcast_to(sums[1], (8, 128)) + EPSILON
    coefficient = jnp.broadcast_to(sums[0], (8, 128)) / denominator
    row_cross = -jnp.broadcast_to(sums[2], (8, 128)) / denominator
    row_square = -2.0 * row_cross * coefficient
    row_model = row_cross + row_square
    spare = coefficient - 1.0

    def adjoint(at, blocks, other):
        entering = CLOSE * (other + AROUND * carry(blocks))
        g2[0, at] = entering
        for p in range(RING - 1):
            entering = blocks[p] + STEP * entering
            g2[p + 1, at] = entering
        return spread(g2, ag2, at)

    def coarse_part(buf, *p):
        return (spare * buf[(*p, slice(6, 9))] - row_model * buf[(*p, slice(9, 12))]
                - row_cross * buf[(*p, slice(12, 15))])

    arrive([over_cot] + over2[:2])
    last = adjoint(slice(3, 9), [rbc[p] + row_cross * rb2[p, 0:6] for p in range(RING)],
                   zbc[...] + row_cross * zb2[0:6])
    arrive(over2[2:])
    last = last + adjoint(slice(0, 3), [coarse_part(rb2, p) for p in range(RING)], coarse_part(zb2))

    def wide(values):
        return jnp.concatenate([values, values], axis=-1)

    coefficient, row_cross, row_square, row_model, spare = (
        wide(coefficient), wide(row_cross), wide(row_square), wide(row_model), wide(spare))
    for a in range(3):
        for i in range(CELLS):
            back[0, a, i] = spare * back[0, a, i] - row_model * back[1, a, i] - row_cross * back[2, a, i]
    for k in range(6):
        for i in range(CELLS):
            leonard, model, bar = leo[k, i], mod[k, i], cot[k, i]
            res[k, i] = leonard - coefficient * model
            weighted = WEIGHTS[k] * row_cross
            leo[k, i] = bar + weighted * model
            mod[k, i] = weighted * leonard - coefficient * bar + (WEIGHTS[k] * row_square) * model
    for copy in copies[:-6]:
        copy.wait_send()
    arrive(last)
    for half in (0, 1):
        lanes = slice(128 * half, 128 * half + 128)
        sums = []
        for a in range(3):
            sums.append(filtered_cells([back[0, a, i, :, lanes] for i in range(CELLS)],
                                       ag2[2 * half, a], ag2[2 * half + 1, a]))
        for k, (a, b) in enumerate(PAIRS):
            pulled = filtered_cells([leo[k, i, :, lanes] for i in range(CELLS)],
                                    ag2[2 * half, 3 + k], ag2[2 * half + 1, 3 + k])
            for i in range(CELLS):
                through = pulled[i] + mod[k, i, :, lanes]
                sums[a][i] = sums[a][i] + through * vel[b, i, :, lanes]
                sums[b][i] = sums[b][i] + through * vel[a, i, :, lanes]
        for a in range(3):
            for i in range(CELLS):
                grad[a, i, :, lanes] = sums[a][i]
    for copy in copies[-6:]:
        copy.wait_send()


def store_both(first, second, first_out, second_out, done):
    copies = [pltpu.make_async_copy(first, first_out, done.at[0]), pltpu.make_async_copy(second, second_out, done.at[1])]
    for copy in copies:
        copy.start()
    for copy in copies:
        copy.wait()


def on_device(velocity, strain, row_bins, cotangent):
    def buf(*shape):
        return pltpu.VMEM(shape, jnp.float32)

    vmem = pl.BlockSpec(memory_space=pltpu.VMEM)
    hbm = pl.BlockSpec(memory_space=pltpu.HBM)
    scratch = [
        buf(3, 4, 8, 256), buf(6, 4, 8, 256), pltpu.SMEM((8,), jnp.int32), buf(6, 4, 8, 256),
        buf(10, 4, 8, 256), buf(4, 4, 8, 256), buf(6, 4, 8, 256), buf(6, 4, 8, 256), buf(3, 3, 4, 8, 256),
        buf(4, 10, 8, 128), buf(4, 10, 8, 128), buf(10, 8, 128), buf(10, 8, 128), buf(4, 10, 8, 128),
        buf(4, 10, 8, 128),
        buf(4, 6, 8, 128), buf(4, 6, 8, 128), buf(6, 8, 128), buf(6, 8, 128),
        buf(4, 15, 8, 128), buf(4, 15, 8, 128), buf(15, 8, 128), buf(15, 8, 128), buf(4, 9, 8, 128),
        buf(4, 9, 8, 128),
        buf(1, 128), buf(4, 1, 128), buf(1, 128), buf(5, 8, 1, 128),
        pltpu.SemaphoreType.DMA((96,)), pltpu.SemaphoreType.DMA((96,)), pltpu.SemaphoreType.DMA((4,)),
        pltpu.SemaphoreType.REGULAR,
    ]
    results = pl.pallas_call(
        kernel,
        out_shape=(
            pltpu.VMEM(strain.shape, jnp.float32),
            pltpu.VMEM(velocity.shape, jnp.float32),
        ),
        in_specs=[hbm, hbm, hbm, hbm],
        out_specs=(vmem, vmem),
        scratch_shapes=scratch,
        compiler_params=pltpu.CompilerParams(
            collective_id=1, has_side_effects=True, vmem_limit_bytes=32 * 1024 * 1024),
        cost_estimate=pl.CostEstimate(flops=3_000_000, bytes_accessed=800_000, transcendentals=8192),
    )(*[pltpu.with_memory_space_constraint(v, pltpu.HBM) for v in (velocity, strain, row_bins, cotangent)])
    return pl.pallas_call(
        store_both,
        out_shape=(pltpu.HBM(strain.shape, jnp.float32), pltpu.HBM(velocity.shape, jnp.float32)),
        in_specs=[vmem, vmem],
        out_specs=(hbm, hbm),
        scratch_shapes=[pltpu.SemaphoreType.DMA((2,))],
    )(*[pltpu.with_memory_space_constraint(v, pltpu.VMEM) for v in results])


def solution(mesh):
    field = P(None, "span", "stream", None)
    return jax.shard_map(
        on_device, mesh=mesh, in_specs=(field, field, P("stream"), field), out_specs=(field, field),
        check_vma=False)
```
